32 devices in a mesh: group: 2 (over x), expert: 4 (over y, core), dp: 4 (over z).
Axes of the slice: x: 2, y: 2, z: 4, core: 2. Of those that a mesh axis runs over, the one named last changes fastest.
Arguments:
- query: bfloat16 [256, 8192], P(('group', 'expert', 'dp')), parts along dimension 0, may hold values from -5 to 5
- key_cache: bfloat16 [256, 4, 256, 128], P(('group', 'expert', 'dp')), parts along dimension 0, may hold values from -5 to 5
- value_cache: bfloat16 [256, 4, 256, 128], P(('group', 'expert', 'dp')), parts along dimension 0, may hold values from -6 to 6
- new_key: bfloat16 [256, 512], P(('group', 'expert', 'dp')), parts along dimension 0, may hold values from -5 to 5
- new_value: bfloat16 [256, 512], P(('group', 'expert', 'dp')), parts along dimension 0, may hold values from -6 to 6
- lengths: int32 [256], P(('group', 'expert', 'dp')), parts along dimension 0, may hold values from 2 to 256, as said below
- residual: bfloat16 [256, 4096], P(('group', 'expert', 'dp')), parts along dimension 0, may hold values from -4 to 4
- out_proj: bfloat16 [8192, 4096], P('expert'), may hold values from -0.5 to 0.5
- norm_gain: float32 [4096], replicated, may hold values from 0.5 to 1.5
- expert_ids: int32 [256, 8], P(('group', 'expert', 'dp')), parts along dimension 0, may hold values from 0 to 15, all different within a row; in each aligned block of 8 rows (0 to 7, 8 to 15, ...) at most 6 rows name the same one
- gate_probs: float32 [256, 8], P(('group', 'expert', 'dp')), parts along dimension 0, may hold values from 0.02 to 1
- w_gate: bfloat16 [16, 4096, 1536], P('expert', None, 'dp'), may hold values from -0.09375 to 0.09375
- w_up: bfloat16 [16, 4096, 1536], P('expert', None, 'dp'), may hold values from -0.09375 to 0.09375
- w_down: bfloat16 [16, 1536, 4096], P('expert', 'dp'), may hold values from -0.625 to 0.625
Outputs:
- layer_out: bfloat16 [256, 4096], P(('group', 'expert', 'dp')), parts along dimension 0
The draws below stay inside these ranges and needn't reach their ends.
There are 2 independent parts, one for each index of `group`. The reference program is written for one: setup_inputs(seed, part) draws one part's arguments, and reference() takes and returns one part's arrays. A program takes and returns all parts, laid end to end along the dimension named above; an argument that names none is the same for every part. Nothing has to cross between parts.
Inputs may be any that keep to these rules, and one draw needn't show every extreme that they name: `lengths`: some row holds 256 cached positions. `expert_ids`: each row names 8 different experts; among the rows of one device no expert is named by more than 6 rows.
All inputs are finite; a program needn't handle non-finite values.
Results may differ from the reference program's by a relative error of at most 0.0074.
Values may be sent and summed in bfloat16 or wider, within the bound.
A program may use at most 128 MiB of HBM per device.

```python
import math
import jax
import jax.numpy as jnp
import numpy as np
from jax import lax

D = 4096
HEADS = 64
KV_HEADS = 4
HEAD_DIM = 128
FF = 1536
TOPK = 8
EXPERTS = 16
ROW_DEV = 8
CACHE = 256
MOST = 6
ROWS = 128


def draw_query(key, part):
    key = jax.random.fold_in(key, 7)
    values = jnp.clip(jax.random.normal(key, (ROWS, HEADS * HEAD_DIM), jnp.float32), -5.0, 5.0)
    return values.astype(jnp.bfloat16)


def draw_key_cache(key, part):
    key = jax.random.fold_in(key, 8)
    shape = (ROWS, KV_HEADS, CACHE, HEAD_DIM)
    values = jnp.clip(jax.random.normal(key, shape, jnp.float32), -5.0, 5.0)
    return values.astype(jnp.bfloat16)


def draw_lengths(key, part):
    key = jax.random.fold_in(key, 9)
    pick_key, length_key = jax.random.split(key)
    drawn = jax.random.randint(length_key, (ROWS,), 2, CACHE + 1)
    longest = jax.random.randint(pick_key, (), 0, ROWS)
    return jnp.where(jnp.arange(ROWS) == longest, CACHE, drawn).astype(jnp.int32)


def steps_of(rng, shape, cuts, least, largest):
    def one(dim, blocks):
        draws = jax.random.uniform(jax.random.fold_in(jax.random.fold_in(rng, 6), dim), (blocks,), jnp.float32, least / len(cuts), largest / len(cuts))
        return jnp.repeat(jnp.exp(draws), shape[dim] // blocks).reshape((-1,) + (1,) * (len(shape) - dim - 1))

    loudness = one(*cuts[0])
    for cut in cuts[1:]:
        loudness = loudness * one(*cut)
    return loudness


def assign_block(stream_key, own, number, rows, count, top, most, lean):
    sequence = jax.random.permutation(stream_key, count)
    packed, common = shares(count, rows * top, most, lean, True), shares(count, rows * top, most, lean, False)
    places = jnp.arange(count)

    def named(sizes, rotation):
        used = int((sizes > 0).sum())
        fixed = max(1, used // 4)
        passed = fixed + (places - fixed + rotation * (used - fixed)) % max(1, count - fixed)
        return jnp.zeros((count,), jnp.int32).at[sequence[jnp.where(places < fixed, places, passed)]].set(jnp.asarray(sizes, jnp.int32))

    sizes = jnp.where(number % 4 == 0, named(packed, number // 4), named(common, number - number // 4 - 1))
    mixed = jax.random.permutation(jax.random.fold_in(own, 3), count)
    donor, receiver = mixed[0:count // 2 * 2:2], mixed[1:count // 2 * 2:2]
    room = jnp.minimum(sizes[donor] - 1, most - sizes[receiver]) // 2
    room = jnp.where((donor == sequence[0]) | (receiver == sequence[0]) | (sizes[receiver] == 0), 0, jnp.maximum(room, 0))
    passed = jax.random.randint(jax.random.fold_in(own, 4), (count // 2,), 0, 1 << 20) % (room + 1)
    sizes = sizes.at[donor].add(-passed).at[receiver].add(passed)
    labels = jnp.searchsorted(jnp.cumsum(sizes), jnp.arange(rows * top), side="right").astype(jnp.int32)
    grid = labels.reshape(top, rows).T
    grid = grid[jax.random.permutation(jax.random.fold_in(own, 1), rows)]
    rotation = jax.random.randint(jax.random.fold_in(own, 2), (rows, 1), 0, top)
    return jnp.take_along_axis(grid, (jnp.arange(top)[None, :] + rotation) % top, axis=1)


def shares(number_of, total, limit, slope, full):
    weights = [(1 << 20) // math.isqrt(standing ** slope) + 1 for standing in range(1, number_of + 1)]
    largest = limit if full else min(limit, max(-(-total // number_of), total * weights[0] // sum(weights)))
    least = 1 if total - largest >= number_of - 1 else 0
    given, spare = [largest] + [least] * (number_of - 1), total - largest - least * (number_of - 1)
    while spare > 0:
        movable = [i for i in range(1, number_of) if given[i] < largest] or [i for i in range(1, number_of) if given[i] < limit]
        mass, remaining = sum([weights[i] for i in movable]), spare
        for i in movable:
            addition = min(limit - given[i], max(1, remaining * weights[i] // mass), spare)
            given[i] = given[i] + addition
            spare = spare - addition
    return np.array(given)


def bell_draw(rng, extent, scale, most, cuts=(), held_as=jnp.bfloat16):
    entries = scale * jax.random.normal(rng, extent, jnp.float32)
    if cuts:
        entries = entries * steps_of(rng, extent, cuts, -0.22, 0.18)
    return jnp.clip(entries, -most, most).astype(held_as)


def setup_inputs(seed: int = 0, part: int = 0) -> dict:
    arg_keys = jax.random.split(jax.random.key(seed), 15)
    own_keys = jax.random.split(jax.random.fold_in(arg_keys[14], part), 15)
    query = draw_query(jax.random.fold_in(jax.random.fold_in(arg_keys[14], part), 71), part)
    key_cache = draw_key_cache(jax.random.fold_in(jax.random.fold_in(arg_keys[14], part), 71), part)
    value_cache = bell_draw(own_keys[2], (ROWS, KV_HEADS, CACHE, HEAD_DIM), 1.0, 6.0, ((0, 16),))
    new_key = bell_draw(own_keys[3], (ROWS, KV_HEADS * HEAD_DIM), 1.0, 5.0, ((0, 16),))
    new_value = bell_draw(own_keys[4], (ROWS, KV_HEADS * HEAD_DIM), 1.0, 6.0, ((0, 16),))
    lengths = draw_lengths(jax.random.fold_in(jax.random.fold_in(arg_keys[14], part), 71), part)
    residual = bell_draw(own_keys[6], (ROWS, D), 0.5, 4.0, ((0, 16),))
    out_proj = bell_draw(arg_keys[7], (HEADS * HEAD_DIM, D), HEAD_DIM ** -0.5, 0.5, ((0, 4),))
    norm_gain = jnp.clip(1.0 + 0.1 * jax.random.normal(arg_keys[8], (D,), jnp.float32), 0.5, 1.5)
    expert_ids_keys = jax.random.split(jax.random.fold_in(own_keys[9], 1), ROWS // ROW_DEV)
    expert_ids_turns = jax.random.permutation(jax.random.fold_in(own_keys[9], 3), ROWS // ROW_DEV)
    expert_ids = jax.vmap(lambda own, number: assign_block(jax.random.fold_in(own_keys[9], 2), own, number, ROW_DEV, EXPERTS, TOPK, MOST, 2))(expert_ids_keys, expert_ids_turns).reshape((ROWS, TOPK))
    gate_probs = jnp.clip(jnp.exp(math.log(1.0) - 3.912023 * jax.random.uniform(own_keys[10], (ROWS, TOPK), jnp.float32) ** steps_of(own_keys[10], (ROWS, TOPK), ((0, 16),), -0.2, 0.2)), 0.02, 1.0)
    w_gate = bell_draw(arg_keys[11], (EXPERTS, D, FF), D ** -0.5, 0.09375, ((0, 4), (2, 4)))
    w_up = bell_draw(arg_keys[12], (EXPERTS, D, FF), D ** -0.5, 0.09375, ((0, 4), (2, 4)))
    w_down = bell_draw(arg_keys[13], (EXPERTS, FF, D), (FF // 16) ** -0.5, 0.625, ((0, 4), (1, 4)))
    return {"query": query, "key_cache": key_cache, "value_cache": value_cache, "new_key": new_key, "new_value": new_value, "lengths": lengths, "residual": residual, "out_proj": out_proj, "norm_gain": norm_gain, "expert_ids": expert_ids, "gate_probs": gate_probs, "w_gate": w_gate, "w_up": w_up, "w_down": w_down}


EPS = 1e-06

def attend_block(blocks):
    query, key_cache, value_cache, new_key, new_value, lengths = blocks
    row_count = query.shape[0]
    per_group = HEADS // KV_HEADS
    queries = query.astype(jnp.float32).reshape(row_count, KV_HEADS, per_group, HEAD_DIM)
    scaling = 1.0 / math.sqrt(HEAD_DIM)
    scores = jnp.einsum('rkgd,rkcd->rkgc', queries, key_cache.astype(jnp.float32)) * scaling
    fresh_keys = new_key.astype(jnp.float32).reshape(row_count, KV_HEADS, HEAD_DIM)
    self_score = jnp.einsum('rkgd,rkd->rkg', queries, fresh_keys) * scaling
    usable = jnp.arange(CACHE, dtype=jnp.int32)[None, :] < lengths[:, None]
    scores = jnp.where(usable[:, None, None, :], scores, -jnp.inf)
    highest = jnp.maximum(lax.optimization_barrier(jnp.max(scores, axis=-1)), self_score)
    exponent = jnp.exp(scores - highest[..., None])
    self_exp = jnp.exp(self_score - highest)
    denominator = lax.optimization_barrier(jnp.sum(exponent, axis=-1)) + self_exp
    weights = lax.optimization_barrier((exponent / denominator[..., None]).astype(jnp.bfloat16)).astype(jnp.float32)
    self_weight = lax.optimization_barrier((self_exp / denominator).astype(jnp.bfloat16)).astype(jnp.float32)
    fresh_values = new_value.astype(jnp.float32).reshape(row_count, KV_HEADS, HEAD_DIM)
    attended = jnp.einsum('rkgc,rkcd->rkgd', weights, value_cache.astype(jnp.float32))
    attended = attended + self_weight[..., None] * fresh_values[:, :, None, :]
    return attended.astype(jnp.bfloat16).reshape(row_count, HEADS * HEAD_DIM)

def routing(expert_ids, gate_probs):
    normalized = gate_probs / lax.optimization_barrier(jnp.sum(gate_probs, axis=-1, keepdims=True))
    matches = expert_ids[:, :, None] == jnp.arange(EXPERTS, dtype=jnp.int32)[None, None, :]
    return lax.optimization_barrier(jnp.sum(jnp.where(matches, normalized[:, :, None], 0.0), axis=1)).astype(jnp.bfloat16)

def reference(query, key_cache, value_cache, new_key, new_value, lengths, residual, out_proj, norm_gain, expert_ids, gate_probs, w_gate, w_up, w_down):
    block_count = ROWS // ROW_DEV

    def split_rows(array):
        return array.reshape((block_count, ROW_DEV) + array.shape[1:])
    pieces = (split_rows(query), split_rows(key_cache), split_rows(value_cache), split_rows(new_key), split_rows(new_value), split_rows(lengths))
    attended = lax.map(attend_block, pieces).reshape(ROWS, HEADS * HEAD_DIM)
    projected = jnp.dot(attended, out_proj, preferred_element_type=jnp.float32)
    hidden = (residual.astype(jnp.float32) + projected).astype(jnp.bfloat16)
    hidden_wide = hidden.astype(jnp.float32)
    mean_square = lax.optimization_barrier(jnp.mean(hidden_wide * hidden_wide, axis=-1, keepdims=True))
    normed = (hidden_wide * lax.rsqrt(mean_square + EPS) * norm_gain).astype(jnp.bfloat16)
    weighting = routing(expert_ids, gate_probs)

    def one_expert(running, expert_index):
        gate_out = jnp.dot(normed, w_gate[expert_index], preferred_element_type=jnp.float32)
        up_out = jnp.dot(normed, w_up[expert_index], preferred_element_type=jnp.float32)
        column = lax.dynamic_slice_in_dim(weighting, expert_index, 1, 1).astype(jnp.float32)
        activated = (jax.nn.silu(gate_out) * up_out * column).astype(jnp.bfloat16)
        return (running + jnp.dot(activated, w_down[expert_index], preferred_element_type=jnp.float32), None)
    expert_sum, unused = lax.scan(one_expert, jnp.zeros((ROWS, D), jnp.float32), jnp.arange(EXPERTS, dtype=jnp.int32))
    return (hidden_wide + expert_sum).astype(jnp.bfloat16)
```

```python
import functools
import math

import jax
import jax.numpy as jnp
from jax import lax
from jax.experimental import pallas as pl
from jax.experimental.pallas import tpu as pltpu
from jax.sharding import PartitionSpec as P

EPS = 1e-06


def attend(query, key_cache, value_cache, new_key, new_value, lengths):
    row_count = query.shape[0]
    kv_count = key_cache.shape[1]
    cache_len = key_cache.shape[2]
    head_size = key_cache.shape[3]
    per_group = query.shape[1] // (kv_count * head_size)
    queries = query.reshape(row_count, kv_count, per_group, head_size)
    scaling = 1.0 / math.sqrt(head_size)
    scores = (
        jnp.einsum("rkgd,rkcd->rkgc", queries, key_cache, preferred_element_type=jnp.float32)
        * scaling
    )
    fresh_keys = new_key.reshape(row_count, kv_count, head_size)
    self_score = (
        jnp.einsum("rkgd,rkd->rkg", queries, fresh_keys, preferred_element_type=jnp.float32)
        * scaling
    )
    usable = jnp.arange(cache_len, dtype=jnp.int32)[None, :] < lengths[:, None]
    scores = jnp.where(usable[:, None, None, :], scores, -jnp.inf)
    highest = jnp.maximum(jnp.max(scores, axis=-1), self_score)
    exponent = jnp.exp(scores - highest[..., None])
    self_exp = jnp.exp(self_score - highest)
    denominator = jnp.sum(exponent, axis=-1) + self_exp
    weights = (exponent / denominator[..., None]).astype(jnp.bfloat16)
    self_weight = lax.optimization_barrier((self_exp / denominator).astype(jnp.bfloat16)).astype(
        jnp.float32
    )
    fresh_values = new_value.astype(jnp.float32).reshape(row_count, kv_count, head_size)
    attended = jnp.einsum(
        "rkgc,rkcd->rkgd", weights, value_cache, preferred_element_type=jnp.float32
    )
    attended = attended + self_weight[..., None] * fresh_values[:, :, None, :]
    return attended.astype(jnp.bfloat16).reshape(row_count, per_group * kv_count * head_size)


def routing(expert_ids, gate_probs, expert_total):
    normalized = gate_probs / jnp.sum(gate_probs, axis=-1, keepdims=True)
    matches = expert_ids[:, :, None] == jnp.arange(expert_total, dtype=jnp.int32)[None, None, :]
    return jnp.sum(jnp.where(matches, normalized[:, :, None], 0.0), axis=1).astype(jnp.bfloat16)


def expert_apply(row_block, weight_block, w_gate, w_up):
    gate_out = jnp.einsum("md,kdf->mkf", row_block, w_gate, preferred_element_type=jnp.float32)
    up_out = jnp.einsum("md,kdf->mkf", row_block, w_up, preferred_element_type=jnp.float32)
    activated = (
        jax.nn.silu(gate_out) * up_out * weight_block.astype(jnp.float32)[:, :, None]
    ).astype(jnp.bfloat16)
    return activated.reshape(row_block.shape[0], -1)


def per_device(
    query,
    key_cache,
    value_cache,
    new_key,
    new_value,
    lengths,
    residual,
    out_proj,
    norm_gain,
    expert_ids,
    gate_probs,
    w_gate,
    w_up,
    w_down,
):
    width = residual.shape[1]
    local_experts = w_gate.shape[0]
    n_expert = lax.axis_size("expert")
    down_flat = w_down.reshape(-1, width)
    attended = attend(query, key_cache, value_cache, new_key, new_value, lengths)
    received = lax.all_to_all(attended, "expert", split_axis=1, concat_axis=0, tiled=True)
    projected = lax.psum_scatter(
        jnp.dot(received, out_proj, preferred_element_type=jnp.float32),
        "expert",
        scatter_dimension=0,
        tiled=True,
    )
    hidden = (residual.astype(jnp.float32) + projected).astype(jnp.bfloat16)
    hidden_wide = hidden.astype(jnp.float32)
    mean_square = jnp.mean(hidden_wide * hidden_wide, axis=-1, keepdims=True)
    normed = (hidden_wide * lax.rsqrt(mean_square + EPS) * norm_gain).astype(jnp.bfloat16)
    expert_total = local_experts * n_expert
    weighting = routing(expert_ids, gate_probs, expert_total)
    all_rows, all_weighting = (
        lax.all_gather(normed, ("expert", "dp"), axis=0, tiled=True),
        lax.all_gather(weighting, ("expert", "dp"), axis=0, tiled=True),
    )
    first_expert = lax.axis_index("expert") * local_experts
    local_weighting = lax.dynamic_slice_in_dim(all_weighting, first_expert, local_experts, 1)
    activated = expert_apply(all_rows, local_weighting, w_gate, w_up)
    expert_sum = lax.psum_scatter(
        jnp.dot(activated, down_flat, preferred_element_type=jnp.float32),
        ("expert", "dp"),
        scatter_dimension=0,
        tiled=True,
    )
    return (hidden_wide + expert_sum).astype(jnp.bfloat16)


MESH = pl.DeviceIdType.MESH
F32 = jnp.float32
BF16 = jnp.bfloat16
CHUNKS = 4
SIDE = 128
MIB = 1 << 20


def fused_kernel(
    n_expert,
    n_dp,
    query,
    key_cache,
    value_cache,
    new_key,
    new_value,
    lengths,
    residual,
    out_proj,
    norm_gain,
    expert_ids,
    gate_probs,
    w_gate,
    w_up,
    w_down,
    out,
    k_buf,
    v_buf,
    wo_buf,
    gu_buf,
    q_rows,
    o_rows,
    att_send,
    att_recv,
    proj_send,
    proj_recv,
    proj_own,
    hidden_buf,
    gathered,
    acts,
    part,
    s1,
    r1,
    s2,
    r2,
    s3,
    r3,
    kv_sem,
    wo_sem,
    gu_sem,
    wd_sem,
    att_ssem,
    att_rsem,
    proj_ssem,
    proj_rsem,
    gat_ssem,
    gat_rsem,
    s1_sem,
    r1_sem,
    s2_sem,
    r2_sem,
    s3_sem,
    r3_sem,
):
    rows, kv_count, cache_len, head_size = key_cache.shape
    per_group = query.shape[1] // (kv_count * head_size)
    width = residual.shape[1]
    feat = att_send.shape[2]
    local_experts, _, ff = w_gate.shape
    chunk = width // CHUNKS
    e = lax.axis_index("expert")
    z = lax.axis_index("dp")
    core = lax.rem(e, 2)
    y = lax.div(e, 2)
    mate = e + 1 - 2 * core
    across = lax.rem(e + 2, 4)

    barrier = pltpu.get_barrier_semaphore()
    for step in range(1, n_expert):
        pl.semaphore_signal(
            barrier, inc=1, device_id={"expert": lax.rem(e + step, n_expert)}, device_id_type=MESH
        )
    for step in range(1, n_dp):
        pl.semaphore_signal(
            barrier, inc=1, device_id={"dp": lax.rem(z + step, n_dp)}, device_id_type=MESH
        )

    heads = [lax.rem(e + 1 + step, n_expert) for step in range(n_expert)]
    kv_copies = []
    for step, k in enumerate(heads):
        kc = pltpu.make_async_copy(key_cache.at[:, k], k_buf.at[step], kv_sem.at[0, step])
        vc = pltpu.make_async_copy(value_cache.at[:, k], v_buf.at[step], kv_sem.at[1, step])
        kc.start()
        vc.start()
        kv_copies.append((kc, vc))
    wo_copies = []
    for n in range(CHUNKS):
        cols = pl.ds(n * chunk, chunk)
        wc = pltpu.make_async_copy(out_proj.at[:, cols], wo_buf.at[:, cols], wo_sem.at[n])
        wc.start()
        wo_copies.append(wc)
    gu_copies = []
    for j in range(local_experts):
        for t, w in enumerate((w_gate, w_up)):
            gc = pltpu.make_async_copy(
                w.at[j], gu_buf.at[:, pl.ds((2 * j + t) * ff, ff)], gu_sem.at[j, t]
            )
            gc.start()
            gu_copies.append(gc)

    for h in range(kv_count * per_group):
        q_rows[pl.ds(h, rows, stride=kv_count * per_group), :] = query[
            :, h * head_size : (h + 1) * head_size
        ].astype(F32)
    scaling = 1.0 / math.sqrt(head_size)
    place = lax.broadcasted_iota(jnp.int32, (per_group, cache_len), 1)

    att_copies = []
    for step, k in enumerate(heads):
        kv_copies[step][0].wait()
        lanes = pl.ds(pl.multiple_of(k * head_size, head_size), head_size)
        fresh_k = new_key[:, lanes].astype(F32)
        fresh_v = new_value[:, lanes].astype(F32)
        scores, selfs = [], []
        for r in range(rows):
            start = pl.multiple_of(r * kv_count * per_group + k * per_group, per_group)
            q = q_rows[pl.ds(start, per_group), :]
            score = lax.dot_general(
                q.astype(BF16),
                k_buf[step, r],
                (((1,), (1,)), ((), ())),
                preferred_element_type=F32,
            )
            score = jnp.where(place < lengths[r], score * scaling, -jnp.inf)
            scores.append(score)
            selfs.append(jnp.sum(q * fresh_k[r : r + 1], axis=-1, keepdims=True) * scaling)
        score = jnp.concatenate(scores, axis=0)
        self_score = jnp.concatenate(selfs, axis=0)
        highest = jnp.maximum(jnp.max(score, axis=-1, keepdims=True), self_score)
        exponent = jnp.exp(score - highest)
        self_exp = jnp.exp(self_score - highest)
        denominator = jnp.sum(exponent, axis=-1, keepdims=True) + self_exp
        weights = (exponent / denominator).astype(BF16)
        self_weight = (self_exp / denominator).astype(BF16).astype(F32)
        kv_copies[step][1].wait()
        for r in range(rows):
            band = slice(r * per_group, (r + 1) * per_group)
            o_rows[band, :] = (
                jnp.dot(weights[band], v_buf[step, r], preferred_element_type=F32)
                + self_weight[band] * fresh_v[r : r + 1]
            )
        if step == 0:
            pl.semaphore_wait(barrier, n_expert + n_dp - 2)
        last = step == n_expert - 1
        target = att_recv.at[e] if last else att_send.at[step]
        for h in range(per_group):
            target[:, h * head_size : (h + 1) * head_size] = o_rows[
                pl.ds(h, rows, stride=per_group), :
            ].astype(BF16)
        if not last:
            copy = pltpu.make_async_remote_copy(
                src_ref=att_send.at[step],
                dst_ref=att_recv.at[e],
                send_sem=att_ssem.at[step],
                recv_sem=att_rsem.at[e],
                device_id={"expert": k},
                device_id_type=MESH,
            )
            copy.start()
            att_copies.append(copy)

    probs = gate_probs[...]
    probs = probs / jnp.sum(probs, axis=-1, keepdims=True)
    ids = expert_ids[...]
    side_place = lax.broadcasted_iota(jnp.int32, (rows, SIDE), 1)
    weighting = jnp.zeros((rows, SIDE), F32)
    for t in range(ids.shape[1]):
        weighting = weighting + jnp.where(side_place == ids[:, t : t + 1], probs[:, t : t + 1], 0.0)
    mine = e * n_dp + z
    gathered[mine, :, width:] = weighting.astype(BF16)

    for step in range(n_expert - 1):
        src = lax.rem(e + 1 + step, n_expert)
        pltpu.make_async_remote_copy(
            src_ref=att_send.at[step],
            dst_ref=att_recv.at[src],
            send_sem=att_ssem.at[step],
            recv_sem=att_rsem.at[src],
            device_id={"expert": src},
            device_id_type=MESH,
        ).wait_recv()
    left = jnp.concatenate([att_recv[i].astype(F32) for i in range(n_expert)], axis=0).astype(BF16)
    proj_copies = []
    tile = 512
    for n in range(CHUNKS):
        wo_copies[n].wait()

        @pl.loop(0, chunk // tile)
        def _(t):
            cols = pl.ds(pl.multiple_of(n * chunk + t * tile, tile), tile)
            product = jnp.dot(left, wo_buf[:, cols], preferred_element_type=F32)
            for i in range(n_expert):
                proj_own[i, :, cols] = product[i * rows : (i + 1) * rows]

        cols = pl.ds(n * chunk, chunk)
        for step in range(n_expert - 1):
            dst = lax.rem(e + 1 + step, n_expert)
            proj_send[n, step] = proj_own[dst, :, cols].astype(BF16)
            copy = pltpu.make_async_remote_copy(
                src_ref=proj_send.at[n, step],
                dst_ref=proj_recv.at[n, step],
                send_sem=proj_ssem.at[n, step],
                recv_sem=proj_rsem.at[n, step],
                device_id={"expert": dst},
                device_id_type=MESH,
            )
            copy.start()
            proj_copies.append(copy)
    wd_copies = []
    for j in range(local_experts):
        wc = pltpu.make_async_copy(w_down.at[j], wo_buf.at[pl.ds(j * ff, ff), :], wd_sem.at[j])
        wc.start()
        wd_copies.append(wc)

    squares = jnp.zeros((rows, 1), F32)
    for n in range(CHUNKS):
        cols = slice(n * chunk, (n + 1) * chunk)
        total = residual[:, cols].astype(F32) + proj_own[e, :, cols]
        for step in range(n_expert - 1):
            proj_copies[n * (n_expert - 1) + step].wait_recv()
            total = total + proj_recv[n, step].astype(F32)
        total = total.astype(BF16).astype(F32)
        hidden_buf[:, cols] = total
        squares = squares + jnp.sum(total * total, axis=-1, keepdims=True)
    inverse = lax.rsqrt(squares * (1.0 / width) + EPS)
    for n in range(CHUNKS):
        cols = slice(n * chunk, (n + 1) * chunk)
        gathered[mine, :, cols] = (hidden_buf[:, cols] * inverse * norm_gain[:, cols]).astype(BF16)

    def give(block, slot, device):
        copy = pltpu.make_async_remote_copy(
            src_ref=gathered.at[block],
            dst_ref=gathered.at[block],
            send_sem=gat_ssem.at[slot],
            recv_sem=gat_rsem.at[block],
            device_id=device,
            device_id_type=MESH,
        )
        copy.start()
        return copy

    def arrive(block):
        pltpu.make_async_remote_copy(
            src_ref=gathered.at[block],
            dst_ref=gathered.at[block],
            send_sem=gat_ssem.at[0],
            recv_sem=gat_rsem.at[block],
            device_id={"expert": mate},
            device_id_type=MESH,
        ).wait_recv()

    gives = []

    def pass_on(block, device):
        gives.append(give(block, len(gives), device))

    pass_on(mine, {"expert": across})
    for step in range(1, n_dp):
        pass_on(mine, {"dp": lax.rem(z + step, n_dp)})
    pass_on(mine, {"expert": mate})
    for step in range(n_dp):
        there = lax.rem(z + n_dp - step, n_dp)
        if step:
            block = e * n_dp + there
            arrive(block)
            pass_on(block, {"expert": across})
            pass_on(block, {"expert": mate})
        block = across * n_dp + there
        arrive(block)
        pass_on(block, {"expert": mate})
    mate_across = lax.rem(mate + 2, 4)
    for step in range(n_dp):
        there = lax.rem(z + n_dp - step, n_dp)
        arrive(mate * n_dp + there)
        arrive(mate_across * n_dp + there)

    blocks = n_expert * n_dp
    all_rows = blocks * rows
    for copy in gu_copies:
        copy.wait()
    all_weights = gathered[:, :, width:].astype(F32).reshape(all_rows, SIDE)
    all_place = lax.broadcasted_iota(jnp.int32, (all_rows, SIDE), 1)

    @pl.loop(0, local_experts)
    def _(j):
        cols = pl.ds(pl.multiple_of(j * (2 * ff), 2 * ff), 2 * ff)
        total = jnp.zeros((all_rows, 2 * ff), F32)
        for n in range(CHUNKS):
            ks = slice(n * chunk, (n + 1) * chunk)
            x = gathered[:, :, ks].reshape(all_rows, chunk)
            total = total + jnp.dot(x, gu_buf[ks, cols], preferred_element_type=F32)
        gate_out = total[:, :ff]
        up_out = total[:, ff:]
        column = jnp.sum(
            jnp.where(all_place == e * local_experts + j, all_weights, 0.0), axis=-1, keepdims=True
        )
        activated = gate_out / (1.0 + jnp.exp(-gate_out)) * up_out * column
        acts[:, pl.ds(pl.multiple_of(j * ff, ff), ff)] = activated.astype(BF16)

    for copy in wd_copies:
        copy.wait()

    def stage(send, recv, ssem, rsem, device):
        copy = pltpu.make_async_remote_copy(
            src_ref=send, dst_ref=recv, send_sem=ssem, recv_sem=rsem, device_id=device, device_id_type=MESH
        )
        copy.start()
        return copy

    c1, c2, c3 = [], [], []

    def down(n):
        @pl.loop(0, chunk // tile)
        def _(t):
            cols = pl.ds(pl.multiple_of(n * chunk + t * tile, tile), tile)
            here = pl.ds(pl.multiple_of(t * tile, tile), tile)
            product = jnp.dot(
                acts[...], wo_buf[: local_experts * ff, cols], preferred_element_type=F32
            )
            part[n, :, :, :, :, here] = product.reshape(2, 2, n_dp, rows, tile)

        s1[n] = part[n, :, 1 - core].astype(BF16)
        c1.append(stage(s1.at[n], r1.at[n], s1_sem.at[n], r1_sem.at[n], {"expert": mate}))

    def second(n):
        c1[n].wait_recv()
        s2[n] = (part[n, 1 - y, core] + r1[n, 1 - y].astype(F32)).astype(BF16)
        c2.append(stage(s2.at[n], r2.at[n], s2_sem.at[n], r2_sem.at[n], {"expert": across}))
        part[n, y, core] = part[n, y, core] + r1[n, y].astype(F32)

    def third(n):
        c2[n].wait_recv()
        for step in range(1, n_dp):
            there = lax.rem(z + step, n_dp)
            s3[n, step - 1] = (part[n, y, core, there] + r2[n, there].astype(F32)).astype(BF16)
            c3.append(
                stage(
                    s3.at[n, step - 1],
                    r3.at[n, step - 1],
                    s3_sem.at[n, step - 1],
                    r3_sem.at[n, step - 1],
                    {"dp": there},
                )
            )

    def finish(n):
        cols = slice(n * chunk, (n + 1) * chunk)
        total = part[n, y, core, z] + r2[n, z].astype(F32)
        for step in range(n_dp - 1):
            c3[n * (n_dp - 1) + step].wait_recv()
            total = total + r3[n, step].astype(F32)
        out[:, cols] = (hidden_buf[:, cols] + total).astype(BF16)

    for n in range(CHUNKS + 2):
        if n < CHUNKS:
            down(n)
        if 0 <= n - 1 < CHUNKS:
            second(n - 1)
        if 0 <= n - 2 < CHUNKS:
            third(n - 2)
    for n in range(CHUNKS):
        finish(n)
    for copy in att_copies + proj_copies + gives + c1 + c2 + c3:
        copy.wait_send()


def per_device_fused(sizes, *args):
    n_expert, n_dp = sizes["expert"], sizes["dp"]
    query, key_cache, w_gate = args[0], args[1], args[11]
    residual, out_proj = args[6], args[7]
    rows, kv_count, cache_len, head_size = key_cache.shape
    width = residual.shape[1]
    local_experts, _, ff = w_gate.shape
    feat = out_proj.shape[0]
    weight_bytes = 2 * (out_proj.size + 2 * w_gate.size + 2 * key_cache.size)
    fits = (
        n_expert == 4
        and kv_count == n_expert
        and ff % 128 == 0
        and local_experts * ff <= feat
        and rows == 8
        and weight_bytes <= 48 * MIB
    )
    if not fits:
        return per_device(*args)
    per_group = query.shape[1] // (kv_count * head_size)
    blocks = n_expert * n_dp
    chunk = width // CHUNKS
    dma = pltpu.SemaphoreType.DMA
    vmem, anyspace = pl.BlockSpec(memory_space=pltpu.VMEM), pl.BlockSpec(memory_space=pl.ANY)
    smem = pl.BlockSpec(memory_space=pltpu.SMEM)
    specs = [vmem, anyspace, anyspace, vmem, vmem, smem, vmem, anyspace, vmem, vmem, vmem]
    specs += [anyspace] * 3
    operands = list(args)
    operands[8] = args[8].reshape(1, width)
    flops = 2 * blocks * rows * 3 * w_gate.size + 2 * n_expert * rows * out_proj.size
    return pl.pallas_call(
        functools.partial(fused_kernel, n_expert, n_dp),
        out_shape=jax.ShapeDtypeStruct((rows, width), BF16),
        in_specs=specs,
        out_specs=vmem,
        scratch_shapes=[
            pltpu.VMEM((kv_count, rows, cache_len, head_size), BF16),
            pltpu.VMEM((kv_count, rows, cache_len, head_size), BF16),
            pltpu.VMEM((feat, width), BF16),
            pltpu.VMEM((width, 2 * local_experts * ff), BF16),
            pltpu.VMEM((rows * kv_count * per_group, head_size), F32),
            pltpu.VMEM((rows * per_group, head_size), F32),
            pltpu.VMEM((n_expert - 1, rows, feat), BF16),
            pltpu.VMEM((n_expert, rows, feat), BF16),
            pltpu.VMEM((CHUNKS, n_expert - 1, rows, chunk), BF16),
            pltpu.VMEM((CHUNKS, n_expert - 1, rows, chunk), BF16),
            pltpu.VMEM((n_expert, rows, width), F32),
            pltpu.VMEM((rows, width), F32),
            pltpu.VMEM((blocks, rows, width + SIDE), BF16),
            pltpu.VMEM((blocks * rows, local_experts * ff), BF16),
            pltpu.VMEM((CHUNKS, 2, 2, n_dp, rows, chunk), F32),
            pltpu.VMEM((CHUNKS, 2, n_dp, rows, chunk), BF16),
            pltpu.VMEM((CHUNKS, 2, n_dp, rows, chunk), BF16),
            pltpu.VMEM((CHUNKS, n_dp, rows, chunk), BF16),
            pltpu.VMEM((CHUNKS, n_dp, rows, chunk), BF16),
            pltpu.VMEM((CHUNKS, n_dp - 1, rows, chunk), BF16),
            pltpu.VMEM((CHUNKS, n_dp - 1, rows, chunk), BF16),
            dma((2, n_expert)),
            dma((CHUNKS,)),
            dma((local_experts, 2)),
            dma((local_experts,)),
            dma((n_expert - 1,)),
            dma((n_expert,)),
            dma((CHUNKS, n_expert - 1)),
            dma((CHUNKS, n_expert - 1)),
            dma((4 * n_dp,)),
            dma((blocks,)),
            dma((CHUNKS,)),
            dma((CHUNKS,)),
            dma((CHUNKS,)),
            dma((CHUNKS,)),
            dma((CHUNKS, n_dp - 1)),
            dma((CHUNKS, n_dp - 1)),
        ],
        compiler_params=pltpu.CompilerParams(
            collective_id=0, has_side_effects=True, vmem_limit_bytes=60 * MIB
        ),
        cost_estimate=pl.CostEstimate(
            flops=flops,
            bytes_accessed=2 * (out_proj.size + 3 * w_gate.size + 2 * key_cache.size),
            transcendentals=0,
        ),
    )(*operands)


def solution(mesh):
    return jax.shard_map(
        functools.partial(per_device_fused, dict(mesh.shape)),
        mesh=mesh,
        in_specs=(
            P(("group", "expert", "dp"), None),
            P(("group", "expert", "dp"), None, None, None),
            P(("group", "expert", "dp"), None, None, None),
            P(("group", "expert", "dp"), None),
            P(("group", "expert", "dp"), None),
            P(("group", "expert", "dp")),
            P(("group", "expert", "dp"), None),
            P("expert", None),
            P(),
            P(("group", "expert", "dp"), None),
            P(("group", "expert", "dp"), None),
            P("expert", None, "dp"),
            P("expert", None, "dp"),
            P("expert", "dp", None),
        ),
        out_specs=P(("group", "expert", "dp"), None),
        check_vma=False,
    )
```

```python
import functools
import math

import jax
import jax.numpy as jnp
from jax import lax
from jax.experimental import pallas as pl
from jax.experimental.pallas import tpu as pltpu
from jax.sharding import PartitionSpec as P

EPS = 1e-06


def attend(query, key_cache, value_cache, new_key, new_value, lengths):
    row_count = query.shape[0]
    kv_count = key_cache.shape[1]
    cache_len = key_cache.shape[2]
    head_size = key_cache.shape[3]
    per_group = query.shape[1] // (kv_count * head_size)
    queries = query.reshape(row_count, kv_count, per_group, head_size)
    scaling = 1.0 / math.sqrt(head_size)
    scores = (
        jnp.einsum("rkgd,rkcd->rkgc", queries, key_cache, preferred_element_type=jnp.float32)
        * scaling
    )
    fresh_keys = new_key.reshape(row_count, kv_count, head_size)
    self_score = (
        jnp.einsum("rkgd,rkd->rkg", queries, fresh_keys, preferred_element_type=jnp.float32)
        * scaling
    )
    usable = jnp.arange(cache_len, dtype=jnp.int32)[None, :] < lengths[:, None]
    scores = jnp.where(usable[:, None, None, :], scores, -jnp.inf)
    highest = jnp.maximum(jnp.max(scores, axis=-1), self_score)
    exponent = jnp.exp(scores - highest[..., None])
    self_exp = jnp.exp(self_score - highest)
    denominator = jnp.sum(exponent, axis=-1) + self_exp
    weights = (exponent / denominator[..., None]).astype(jnp.bfloat16)
    self_weight = lax.optimization_barrier((self_exp / denominator).astype(jnp.bfloat16)).astype(
        jnp.float32
    )
    fresh_values = new_value.astype(jnp.float32).reshape(row_count, kv_count, head_size)
    attended = jnp.einsum(
        "rkgc,rkcd->rkgd", weights, value_cache, preferred_element_type=jnp.float32
    )
    attended = attended + self_weight[..., None] * fresh_values[:, :, None, :]
    return attended.astype(jnp.bfloat16).reshape(row_count, per_group * kv_count * head_size)


def routing(expert_ids, gate_probs, expert_total):
    normalized = gate_probs / jnp.sum(gate_probs, axis=-1, keepdims=True)
    matches = expert_ids[:, :, None] == jnp.arange(expert_total, dtype=jnp.int32)[None, None, :]
    return jnp.sum(jnp.where(matches, normalized[:, :, None], 0.0), axis=1).astype(jnp.bfloat16)


def expert_apply(row_block, weight_block, w_gate, w_up):
    gate_out = jnp.einsum("md,kdf->mkf", row_block, w_gate, preferred_element_type=jnp.float32)
    up_out = jnp.einsum("md,kdf->mkf", row_block, w_up, preferred_element_type=jnp.float32)
    activated = (
        jax.nn.silu(gate_out) * up_out * weight_block.astype(jnp.float32)[:, :, None]
    ).astype(jnp.bfloat16)
    return activated.reshape(row_block.shape[0], -1)


def per_device(
    query,
    key_cache,
    value_cache,
    new_key,
    new_value,
    lengths,
    residual,
    out_proj,
    norm_gain,
    expert_ids,
    gate_probs,
    w_gate,
    w_up,
    w_down,
):
    width = residual.shape[1]
    local_experts = w_gate.shape[0]
    n_expert = lax.axis_size("expert")
    down_flat = w_down.reshape(-1, width)
    attended = attend(query, key_cache, value_cache, new_key, new_value, lengths)
    received = lax.all_to_all(attended, "expert", split_axis=1, concat_axis=0, tiled=True)
    projected = lax.psum_scatter(
        jnp.dot(received, out_proj, preferred_element_type=jnp.float32),
        "expert",
        scatter_dimension=0,
        tiled=True,
    )
    hidden = (residual.astype(jnp.float32) + projected).astype(jnp.bfloat16)
    hidden_wide = hidden.astype(jnp.float32)
    mean_square = jnp.mean(hidden_wide * hidden_wide, axis=-1, keepdims=True)
    normed = (hidden_wide * lax.rsqrt(mean_square + EPS) * norm_gain).astype(jnp.bfloat16)
    expert_total = local_experts * n_expert
    weighting = routing(expert_ids, gate_probs, expert_total)
    all_rows, all_weighting = (
        lax.all_gather(normed, ("expert", "dp"), axis=0, tiled=True),
        lax.all_gather(weighting, ("expert", "dp"), axis=0, tiled=True),
    )
    first_expert = lax.axis_index("expert") * local_experts
    local_weighting = lax.dynamic_slice_in_dim(all_weighting, first_expert, local_experts, 1)
    activated = expert_apply(all_rows, local_weighting, w_gate, w_up)
    expert_sum = lax.psum_scatter(
        jnp.dot(activated, down_flat, preferred_element_type=jnp.float32),
        ("expert", "dp"),
        scatter_dimension=0,
        tiled=True,
    )
    return (hidden_wide + expert_sum).astype(jnp.bfloat16)


MESH = pl.DeviceIdType.MESH
F32 = jnp.float32
BF16 = jnp.bfloat16
CHUNKS = 4
SIDE = 128
MIB = 1 << 20


def fused_kernel(
    n_expert,
    n_dp,
    query,
    key_cache,
    value_cache,
    new_key,
    new_value,
    lengths,
    residual,
    out_proj,
    norm_gain,
    expert_ids,
    gate_probs,
    w_gate,
    w_up,
    w_down,
    out,
    k_buf,
    v_buf,
    wo_buf,
    gu_buf,
    q_rows,
    o_rows,
    att_send,
    att_recv,
    proj_send,
    proj_recv,
    proj_own,
    hidden_buf,
    gathered,
    gu_half,
    acts,
    part,
    s1,
    r1,
    s2,
    r2,
    s3,
    r3,
    kv_sem,
    wo_sem,
    gu_sem,
    wd_sem,
    att_ssem,
    att_rsem,
    proj_ssem,
    proj_rsem,
    gat_ssem,
    gat_rsem,
    s1_sem,
    r1_sem,
    s2_sem,
    r2_sem,
    s3_sem,
    r3_sem,
):
    rows, kv_count, cache_len, head_size = key_cache.shape
    per_group = query.shape[1] // (kv_count * head_size)
    width = residual.shape[1]
    feat = att_send.shape[2]
    local_experts, _, ff = w_gate.shape
    chunk = width // CHUNKS
    half = width // 2
    e = lax.axis_index("expert")
    z = lax.axis_index("dp")
    core = lax.rem(e, 2)
    y = lax.div(e, 2)
    mate = e + 1 - 2 * core
    across = lax.rem(e + 2, 4)

    barrier = pltpu.get_barrier_semaphore()
    for step in range(1, n_expert):
        pl.semaphore_signal(
            barrier, inc=1, device_id={"expert": lax.rem(e + step, n_expert)}, device_id_type=MESH
        )
    for step in range(1, n_dp):
        pl.semaphore_signal(
            barrier, inc=1, device_id={"dp": lax.rem(z + step, n_dp)}, device_id_type=MESH
        )

    heads = [lax.rem(e + 1 + step, n_expert) for step in range(n_expert)]
    kv_copies = []
    for step, k in enumerate(heads):
        kc = pltpu.make_async_copy(key_cache.at[:, k], k_buf.at[step], kv_sem.at[0, step])
        vc = pltpu.make_async_copy(value_cache.at[:, k], v_buf.at[step], kv_sem.at[1, step])
        kc.start()
        vc.start()
        kv_copies.append((kc, vc))
    wo_copies = []
    for n in range(CHUNKS):
        cols = pl.ds(n * chunk, chunk)
        wc = pltpu.make_async_copy(out_proj.at[:, cols], wo_buf.at[:, cols], wo_sem.at[n])
        wc.start()
        wo_copies.append(wc)
    gu_copies = []
    for j in range(local_experts):
        for t, w in enumerate((w_gate, w_up)):
            gc = pltpu.make_async_copy(
                w.at[j], gu_buf.at[:, pl.ds((2 * j + t) * ff, ff)], gu_sem.at[j, t]
            )
            gc.start()
            gu_copies.append(gc)

    for h in range(kv_count * per_group):
        q_rows[pl.ds(h, rows, stride=kv_count * per_group), :] = query[
            :, h * head_size : (h + 1) * head_size
        ].astype(F32)
    scaling = 1.0 / math.sqrt(head_size)
    place = lax.broadcasted_iota(jnp.int32, (per_group, cache_len), 1)

    att_copies = []
    for step, k in enumerate(heads):
        kv_copies[step][0].wait()
        lanes = pl.ds(pl.multiple_of(k * head_size, head_size), head_size)
        fresh_k = new_key[:, lanes].astype(F32)
        fresh_v = new_value[:, lanes].astype(F32)
        scores, selfs = [], []
        for r in range(rows):
            start = pl.multiple_of(r * kv_count * per_group + k * per_group, per_group)
            q = q_rows[pl.ds(start, per_group), :]
            score = lax.dot_general(
                q.astype(BF16),
                k_buf[step, r],
                (((1,), (1,)), ((), ())),
                preferred_element_type=F32,
            )
            score = jnp.where(place < lengths[r], score * scaling, -jnp.inf)
            scores.append(score)
            selfs.append(jnp.sum(q * fresh_k[r : r + 1], axis=-1, keepdims=True) * scaling)
        score = jnp.concatenate(scores, axis=0)
        self_score = jnp.concatenate(selfs, axis=0)
        highest = jnp.maximum(jnp.max(score, axis=-1, keepdims=True), self_score)
        exponent = jnp.exp(score - highest)
        self_exp = jnp.exp(self_score - highest)
        denominator = jnp.sum(exponent, axis=-1, keepdims=True) + self_exp
        weights = (exponent / denominator).astype(BF16)
        self_weight = (self_exp / denominator).astype(BF16).astype(F32)
        kv_copies[step][1].wait()
        for r in range(rows):
            band = slice(r * per_group, (r + 1) * per_group)
            o_rows[band, :] = (
                jnp.dot(weights[band], v_buf[step, r], preferred_element_type=F32)
                + self_weight[band] * fresh_v[r : r + 1]
            )
        if step == 0:
            pl.semaphore_wait(barrier, n_expert + n_dp - 2)
        last = step == n_expert - 1
        target = att_recv.at[e] if last else att_send.at[step]
        for h in range(per_group):
            target[:, h * head_size : (h + 1) * head_size] = o_rows[
                pl.ds(h, rows, stride=per_group), :
            ].astype(BF16)
        if not last:
            copy = pltpu.make_async_remote_copy(
                src_ref=att_send.at[step],
                dst_ref=att_recv.at[e],
                send_sem=att_ssem.at[step],
                recv_sem=att_rsem.at[e],
                device_id={"expert": k},
                device_id_type=MESH,
            )
            copy.start()
            att_copies.append(copy)

    probs = gate_probs[...]
    probs = probs / jnp.sum(probs, axis=-1, keepdims=True)
    ids = expert_ids[...]
    side_place = lax.broadcasted_iota(jnp.int32, (rows, SIDE), 1)
    weighting = jnp.zeros((rows, SIDE), F32)
    for t in range(ids.shape[1]):
        weighting = weighting + jnp.where(side_place == ids[:, t : t + 1], probs[:, t : t + 1], 0.0)
    mine = e * n_dp + z
    gathered[0, mine, :, half:] = weighting.astype(BF16)
    gathered[1, mine, :, half:] = jnp.zeros((rows, SIDE), BF16)

    for step in range(n_expert - 1):
        src = lax.rem(e + 1 + step, n_expert)
        pltpu.make_async_remote_copy(
            src_ref=att_send.at[step],
            dst_ref=att_recv.at[src],
            send_sem=att_ssem.at[step],
            recv_sem=att_rsem.at[src],
            device_id={"expert": src},
            device_id_type=MESH,
        ).wait_recv()
    left = jnp.concatenate([att_recv[i].astype(F32) for i in range(n_expert)], axis=0).astype(BF16)
    proj_copies = []
    tile = 512
    for n in range(CHUNKS):
        wo_copies[n].wait()

        @pl.loop(0, chunk // tile)
        def _(t):
            cols = pl.ds(pl.multiple_of(n * chunk + t * tile, tile), tile)
            product = jnp.dot(left, wo_buf[:, cols], preferred_element_type=F32)
            for i in range(n_expert):
                proj_own[i, :, cols] = product[i * rows : (i + 1) * rows]

        cols = pl.ds(n * chunk, chunk)
        for step in range(n_expert - 1):
            dst = lax.rem(e + 1 + step, n_expert)
            proj_send[n, step] = proj_own[dst, :, cols].astype(BF16)
            copy = pltpu.make_async_remote_copy(
                src_ref=proj_send.at[n, step],
                dst_ref=proj_recv.at[n, step],
                send_sem=proj_ssem.at[n, step],
                recv_sem=proj_rsem.at[n, step],
                device_id={"expert": dst},
                device_id_type=MESH,
            )
            copy.start()
            proj_copies.append(copy)
    wd_copies = []
    for j in range(local_experts):
        wc = pltpu.make_async_copy(w_down.at[j], wo_buf.at[pl.ds(j * ff, ff), :], wd_sem.at[j])
        wc.start()
        wd_copies.append(wc)

    squares = jnp.zeros((rows, 1), F32)
    for n in range(CHUNKS):
        cols = slice(n * chunk, (n + 1) * chunk)
        total = residual[:, cols].astype(F32) + proj_own[e, :, cols]
        for step in range(n_expert - 1):
            proj_copies[n * (n_expert - 1) + step].wait_recv()
            total = total + proj_recv[n, step].astype(F32)
        total = total.astype(BF16).astype(F32)
        hidden_buf[:, cols] = total
        squares = squares + jnp.sum(total * total, axis=-1, keepdims=True)
    inverse = lax.rsqrt(squares * (1.0 / width) + EPS)
    def give(part_no, block, slot, device):
        copy = pltpu.make_async_remote_copy(
            src_ref=gathered.at[part_no, block],
            dst_ref=gathered.at[part_no, block],
            send_sem=gat_ssem.at[slot],
            recv_sem=gat_rsem.at[part_no, block],
            device_id=device,
            device_id_type=MESH,
        )
        copy.start()
        return copy

    def arrive(part_no, block):
        pltpu.make_async_remote_copy(
            src_ref=gathered.at[part_no, block],
            dst_ref=gathered.at[part_no, block],
            send_sem=gat_ssem.at[0],
            recv_sem=gat_rsem.at[part_no, block],
            device_id={"expert": mate},
            device_id_type=MESH,
        ).wait_recv()

    gives = []

    def pass_on(part_no, block, device):
        gives.append(give(part_no, block, len(gives), device))

    def begin(part_no):
        start = part_no * half
        gathered[part_no, mine, :, :half] = (
            hidden_buf[:, start : start + half] * inverse * norm_gain[:, start : start + half]
        ).astype(BF16)
        pass_on(part_no, mine, {"expert": across})
        for step in range(1, n_dp):
            pass_on(part_no, mine, {"dp": lax.rem(z + step, n_dp)})
        pass_on(part_no, mine, {"expert": mate})

    def forward(part_no, step):
        there = lax.rem(z + n_dp - step, n_dp)
        if step:
            block = e * n_dp + there
            arrive(part_no, block)
            pass_on(part_no, block, {"expert": across})
            pass_on(part_no, block, {"expert": mate})
        block = across * n_dp + there
        arrive(part_no, block)
        pass_on(part_no, block, {"expert": mate})

    mate_across = lax.rem(mate + 2, 4)

    def complete(part_no):
        for step in range(n_dp):
            there = lax.rem(z + n_dp - step, n_dp)
            arrive(part_no, mate * n_dp + there)
            arrive(part_no, mate_across * n_dp + there)

    begin(0)
    begin(1)
    for step in range(n_dp):
        forward(0, step)
    complete(0)

    blocks = n_expert * n_dp
    all_rows = blocks * rows
    all_weights = gathered[0, :, :, half:].astype(F32).reshape(all_rows, SIDE)
    all_place = lax.broadcasted_iota(jnp.int32, (all_rows, SIDE), 1)

    def half_product(part_no, cols):
        total = jnp.zeros((all_rows, 2 * ff), F32)
        for n in range(CHUNKS // 2):
            x = gathered[part_no, :, :, n * chunk : (n + 1) * chunk].reshape(all_rows, chunk)
            first = part_no * half + n * chunk
            total = total + jnp.dot(x, gu_buf[first : first + chunk, cols], preferred_element_type=F32)
        return total

    for step in range(max(local_experts, n_dp)):
        if step < local_experts:
            gu_copies[2 * step].wait()
            gu_copies[2 * step + 1].wait()
            cols = slice(step * 2 * ff, (step + 1) * 2 * ff)
            gu_half[:, cols] = half_product(0, cols)
        if step < n_dp:
            forward(1, step)
    complete(1)

    @pl.loop(0, local_experts)
    def _(j):
        cols = pl.ds(pl.multiple_of(j * (2 * ff), 2 * ff), 2 * ff)
        total = gu_half[:, cols] + half_product(1, cols)
        gate_out = total[:, :ff]
        up_out = total[:, ff:]
        column = jnp.sum(
            jnp.where(all_place == e * local_experts + j, all_weights, 0.0), axis=-1, keepdims=True
        )
        activated = gate_out / (1.0 + jnp.exp(-gate_out)) * up_out * column
        acts[:, pl.ds(pl.multiple_of(j * ff, ff), ff)] = activated.astype(BF16)

    for copy in wd_copies:
        copy.wait()

    def stage(send, recv, ssem, rsem, device):
        copy = pltpu.make_async_remote_copy(
            src_ref=send, dst_ref=recv, send_sem=ssem, recv_sem=rsem, device_id=device, device_id_type=MESH
        )
        copy.start()
        return copy

    c1, c2, c3 = [], [], []

    def down(n):
        @pl.loop(0, chunk // tile)
        def _(t):
            cols = pl.ds(pl.multiple_of(n * chunk + t * tile, tile), tile)
            here = pl.ds(pl.multiple_of(t * tile, tile), tile)
            product = jnp.dot(
                acts[...], wo_buf[: local_experts * ff, cols], preferred_element_type=F32
            )
            part[n, :, :, :, :, here] = product.reshape(2, 2, n_dp, rows, tile)

        s1[n] = part[n, :, 1 - core].astype(BF16)
        c1.append(stage(s1.at[n], r1.at[n], s1_sem.at[n], r1_sem.at[n], {"expert": mate}))

    def second(n):
        c1[n].wait_recv()
        s2[n] = (part[n, 1 - y, core] + r1[n, 1 - y].astype(F32)).astype(BF16)
        c2.append(stage(s2.at[n], r2.at[n], s2_sem.at[n], r2_sem.at[n], {"expert": across}))
        part[n, y, core] = part[n, y, core] + r1[n, y].astype(F32)

    def third(n):
        c2[n].wait_recv()
        for step in range(1, n_dp):
            there = lax.rem(z + step, n_dp)
            s3[n, step - 1] = (part[n, y, core, there] + r2[n, there].astype(F32)).astype(BF16)
            c3.append(
                stage(
                    s3.at[n, step - 1],
                    r3.at[n, step - 1],
                    s3_sem.at[n, step - 1],
                    r3_sem.at[n, step - 1],
                    {"dp": there},
                )
            )

    def finish(n):
        cols = slice(n * chunk, (n + 1) * chunk)
        total = part[n, y, core, z] + r2[n, z].astype(F32)
        for step in range(n_dp - 1):
            c3[n * (n_dp - 1) + step].wait_recv()
            total = total + r3[n, step].astype(F32)
        out[:, cols] = (hidden_buf[:, cols] + total).astype(BF16)

    for n in range(CHUNKS + 2):
        if n < CHUNKS:
            down(n)
        if 0 <= n - 1 < CHUNKS:
            second(n - 1)
        if 0 <= n - 2 < CHUNKS:
            third(n - 2)
    for n in range(CHUNKS):
        finish(n)
    for copy in att_copies + proj_copies + gives + c1 + c2 + c3:
        copy.wait_send()


def per_device_fused(sizes, *args):
    n_expert, n_dp = sizes["expert"], sizes["dp"]
    query, key_cache, w_gate = args[0], args[1], args[11]
    residual, out_proj = args[6], args[7]
    rows, kv_count, cache_len, head_size = key_cache.shape
    width = residual.shape[1]
    local_experts, _, ff = w_gate.shape
    feat = out_proj.shape[0]
    weight_bytes = 2 * (out_proj.size + 2 * w_gate.size + 2 * key_cache.size)
    fits = (
        n_expert == 4
        and kv_count == n_expert
        and ff % 128 == 0
        and local_experts * ff <= feat
        and rows == 8
        and weight_bytes <= 48 * MIB
    )
    if not fits:
        return per_device(*args)
    per_group = query.shape[1] // (kv_count * head_size)
    blocks = n_expert * n_dp
    chunk = width // CHUNKS
    dma = pltpu.SemaphoreType.DMA
    vmem, anyspace = pl.BlockSpec(memory_space=pltpu.VMEM), pl.BlockSpec(memory_space=pl.ANY)
    smem = pl.BlockSpec(memory_space=pltpu.SMEM)
    specs = [vmem, anyspace, anyspace, vmem, vmem, smem, vmem, anyspace, vmem, vmem, vmem]
    specs += [anyspace] * 3
    operands = list(args)
    operands[8] = args[8].reshape(1, width)
    flops = 2 * blocks * rows * 3 * w_gate.size + 2 * n_expert * rows * out_proj.size
    return pl.pallas_call(
        functools.partial(fused_kernel, n_expert, n_dp),
        out_shape=jax.ShapeDtypeStruct((rows, width), BF16),
        in_specs=specs,
        out_specs=vmem,
        scratch_shapes=[
            pltpu.VMEM((kv_count, rows, cache_len, head_size), BF16),
            pltpu.VMEM((kv_count, rows, cache_len, head_size), BF16),
            pltpu.VMEM((feat, width), BF16),
            pltpu.VMEM((width, 2 * local_experts * ff), BF16),
            pltpu.VMEM((rows * kv_count * per_group, head_size), F32),
            pltpu.VMEM((rows * per_group, head_size), F32),
            pltpu.VMEM((n_expert - 1, rows, feat), BF16),
            pltpu.VMEM((n_expert, rows, feat), BF16),
            pltpu.VMEM((CHUNKS, n_expert - 1, rows, chunk), BF16),
            pltpu.VMEM((CHUNKS, n_expert - 1, rows, chunk), BF16),
            pltpu.VMEM((n_expert, rows, width), F32),
            pltpu.VMEM((rows, width), F32),
            pltpu.VMEM((2, blocks, rows, width // 2 + SIDE), BF16),
            pltpu.VMEM((blocks * rows, 2 * local_experts * ff), F32),
            pltpu.VMEM((blocks * rows, local_experts * ff), BF16),
            pltpu.VMEM((CHUNKS, 2, 2, n_dp, rows, chunk), F32),
            pltpu.VMEM((CHUNKS, 2, n_dp, rows, chunk), BF16),
            pltpu.VMEM((CHUNKS, 2, n_dp, rows, chunk), BF16),
            pltpu.VMEM((CHUNKS, n_dp, rows, chunk), BF16),
            pltpu.VMEM((CHUNKS, n_dp, rows, chunk), BF16),
            pltpu.VMEM((CHUNKS, n_dp - 1, rows, chunk), BF16),
            pltpu.VMEM((CHUNKS, n_dp - 1, rows, chunk), BF16),
            dma((2, n_expert)),
            dma((CHUNKS,)),
            dma((local_experts, 2)),
            dma((local_experts,)),
            dma((n_expert - 1,)),
            dma((n_expert,)),
            dma((CHUNKS, n_expert - 1)),
            dma((CHUNKS, n_expert - 1)),
            dma((8 * n_dp,)),
            dma((2, blocks)),
            dma((CHUNKS,)),
            dma((CHUNKS,)),
            dma((CHUNKS,)),
            dma((CHUNKS,)),
            dma((CHUNKS, n_dp - 1)),
            dma((CHUNKS, n_dp - 1)),
        ],
        compiler_params=pltpu.CompilerParams(
            collective_id=0, has_side_effects=True, vmem_limit_bytes=60 * MIB
        ),
        cost_estimate=pl.CostEstimate(
            flops=flops,
            bytes_accessed=2 * (out_proj.size + 3 * w_gate.size + 2 * key_cache.size),
            transcendentals=0,
        ),
    )(*operands)


def solution(mesh):
    return jax.shard_map(
        functools.partial(per_device_fused, dict(mesh.shape)),
        mesh=mesh,
        in_specs=(
            P(("group", "expert", "dp"), None),
            P(("group", "expert", "dp"), None, None, None),
            P(("group", "expert", "dp"), None, None, None),
            P(("group", "expert", "dp"), None),
            P(("group", "expert", "dp"), None),
            P(("group", "expert", "dp")),
            P(("group", "expert", "dp"), None),
            P("expert", None),
            P(),
            P(("group", "expert", "dp"), None),
            P(("group", "expert", "dp"), None),
            P("expert", None, "dp"),
            P("expert", None, "dp"),
            P("expert", "dp", None),
        ),
        out_specs=P(("group", "expert", "dp"), None),
        check_vma=False,
    )
```

```python
import functools
import math

import jax
import jax.numpy as jnp
from jax import lax
from jax.experimental import pallas as pl
from jax.experimental.pallas import tpu as pltpu
from jax.sharding import PartitionSpec as P

EPS = 1e-06


def attend(query, key_cache, value_cache, new_key, new_value, lengths):
    row_count = query.shape[0]
    kv_count = key_cache.shape[1]
    cache_len = key_cache.shape[2]
    head_size = key_cache.shape[3]
    per_group = query.shape[1] // (kv_count * head_size)
    queries = query.reshape(row_count, kv_count, per_group, head_size)
    scaling = 1.0 / math.sqrt(head_size)
    scores = (
        jnp.einsum("rkgd,rkcd->rkgc", queries, key_cache, preferred_element_type=jnp.float32)
        * scaling
    )
    fresh_keys = new_key.reshape(row_count, kv_count, head_size)
    self_score = (
        jnp.einsum("rkgd,rkd->rkg", queries, fresh_keys, preferred_element_type=jnp.float32)
        * scaling
    )
    usable = jnp.arange(cache_len, dtype=jnp.int32)[None, :] < lengths[:, None]
    scores = jnp.where(usable[:, None, None, :], scores, -jnp.inf)
    highest = jnp.maximum(jnp.max(scores, axis=-1), self_score)
    exponent = jnp.exp(scores - highest[..., None])
    self_exp = jnp.exp(self_score - highest)
    denominator = jnp.sum(exponent, axis=-1) + self_exp
    weights = (exponent / denominator[..., None]).astype(jnp.bfloat16)
    self_weight = lax.optimization_barrier((self_exp / denominator).astype(jnp.bfloat16)).astype(
        jnp.float32
    )
    fresh_values = new_value.astype(jnp.float32).reshape(row_count, kv_count, head_size)
    attended = jnp.einsum(
        "rkgc,rkcd->rkgd", weights, value_cache, preferred_element_type=jnp.float32
    )
    attended = attended + self_weight[..., None] * fresh_values[:, :, None, :]
    return attended.astype(jnp.bfloat16).reshape(row_count, per_group * kv_count * head_size)


def routing(expert_ids, gate_probs, expert_total):
    normalized = gate_probs / jnp.sum(gate_probs, axis=-1, keepdims=True)
    matches = expert_ids[:, :, None] == jnp.arange(expert_total, dtype=jnp.int32)[None, None, :]
    return jnp.sum(jnp.where(matches, normalized[:, :, None], 0.0), axis=1).astype(jnp.bfloat16)


def expert_apply(row_block, weight_block, w_gate, w_up):
    gate_out = jnp.einsum("md,kdf->mkf", row_block, w_gate, preferred_element_type=jnp.float32)
    up_out = jnp.einsum("md,kdf->mkf", row_block, w_up, preferred_element_type=jnp.float32)
    activated = (
        jax.nn.silu(gate_out) * up_out * weight_block.astype(jnp.float32)[:, :, None]
    ).astype(jnp.bfloat16)
    return activated.reshape(row_block.shape[0], -1)


def per_device(
    query,
    key_cache,
    value_cache,
    new_key,
    new_value,
    lengths,
    residual,
    out_proj,
    norm_gain,
    expert_ids,
    gate_probs,
    w_gate,
    w_up,
    w_down,
):
    width = residual.shape[1]
    local_experts = w_gate.shape[0]
    n_expert = lax.axis_size("expert")
    down_flat = w_down.reshape(-1, width)
    attended = attend(query, key_cache, value_cache, new_key, new_value, lengths)
    received = lax.all_to_all(attended, "expert", split_axis=1, concat_axis=0, tiled=True)
    projected = lax.psum_scatter(
        jnp.dot(received, out_proj, preferred_element_type=jnp.float32),
        "expert",
        scatter_dimension=0,
        tiled=True,
    )
    hidden = (residual.astype(jnp.float32) + projected).astype(jnp.bfloat16)
    hidden_wide = hidden.astype(jnp.float32)
    mean_square = jnp.mean(hidden_wide * hidden_wide, axis=-1, keepdims=True)
    normed = (hidden_wide * lax.rsqrt(mean_square + EPS) * norm_gain).astype(jnp.bfloat16)
    expert_total = local_experts * n_expert
    weighting = routing(expert_ids, gate_probs, expert_total)
    all_rows, all_weighting = (
        lax.all_gather(normed, ("expert", "dp"), axis=0, tiled=True),
        lax.all_gather(weighting, ("expert", "dp"), axis=0, tiled=True),
    )
    first_expert = lax.axis_index("expert") * local_experts
    local_weighting = lax.dynamic_slice_in_dim(all_weighting, first_expert, local_experts, 1)
    activated = expert_apply(all_rows, local_weighting, w_gate, w_up)
    expert_sum = lax.psum_scatter(
        jnp.dot(activated, down_flat, preferred_element_type=jnp.float32),
        ("expert", "dp"),
        scatter_dimension=0,
        tiled=True,
    )
    return (hidden_wide + expert_sum).astype(jnp.bfloat16)


MESH = pl.DeviceIdType.MESH
F32 = jnp.float32
BF16 = jnp.bfloat16
CHUNKS = 4
SIDE = 128
MIB = 1 << 20


def fused_kernel(
    n_expert,
    n_dp,
    query,
    key_cache,
    value_cache,
    new_key,
    new_value,
    lengths,
    residual,
    out_proj,
    norm_gain,
    expert_ids,
    gate_probs,
    w_gate,
    w_up,
    w_down,
    out,
    k_buf,
    v_buf,
    wo_buf,
    gu_buf,
    q_rows,
    o_rows,
    att_send,
    att_recv,
    proj_send,
    proj_recv,
    proj_own,
    hidden_buf,
    gathered,
    acts,
    part,
    s1,
    r1,
    s2,
    r2,
    s3,
    r3,
    kv_sem,
    wo_sem,
    gu_sem,
    wd_sem,
    att_ssem,
    att_rsem,
    proj_ssem,
    proj_rsem,
    gat_ssem,
    gat_rsem,
    s1_sem,
    r1_sem,
    s2_sem,
    r2_sem,
    s3_sem,
    r3_sem,
):
    rows, kv_count, cache_len, head_size = key_cache.shape
    per_group = query.shape[1] // (kv_count * head_size)
    width = residual.shape[1]
    feat = att_send.shape[2]
    local_experts, _, ff = w_gate.shape
    chunk = width // CHUNKS
    e = lax.axis_index("expert")
    z = lax.axis_index("dp")
    core = lax.rem(e, 2)
    y = lax.div(e, 2)
    mate = e + 1 - 2 * core
    across = lax.rem(e + 2, 4)

    barrier = pltpu.get_barrier_semaphore()
    for step in range(1, n_expert):
        pl.semaphore_signal(
            barrier, inc=1, device_id={"expert": lax.rem(e + step, n_expert)}, device_id_type=MESH
        )
    for step in range(1, n_dp):
        pl.semaphore_signal(
            barrier, inc=1, device_id={"dp": lax.rem(z + step, n_dp)}, device_id_type=MESH
        )

    heads = [lax.rem(e + 1 + step, n_expert) for step in range(n_expert)]
    kv_copies = []
    for step, k in enumerate(heads):
        kc = pltpu.make_async_copy(key_cache.at[:, k], k_buf.at[step], kv_sem.at[0, step])
        vc = pltpu.make_async_copy(value_cache.at[:, k], v_buf.at[step], kv_sem.at[1, step])
        kc.start()
        vc.start()
        kv_copies.append((kc, vc))
    wo_copies = []
    for n in range(CHUNKS):
        cols = pl.ds(n * chunk, chunk)
        wc = pltpu.make_async_copy(out_proj.at[:, cols], wo_buf.at[:, cols], wo_sem.at[n])
        wc.start()
        wo_copies.append(wc)
    gu_copies = []
    for j in range(local_experts):
        for t, w in enumerate((w_gate, w_up)):
            gc = pltpu.make_async_copy(
                w.at[j], gu_buf.at[:, pl.ds((2 * j + t) * ff, ff)], gu_sem.at[j, t]
            )
            gc.start()
            gu_copies.append(gc)

    for h in range(kv_count * per_group):
        q_rows[pl.ds(h, rows, stride=kv_count * per_group), :] = query[
            :, h * head_size : (h + 1) * head_size
        ].astype(F32)
    scaling = 1.0 / math.sqrt(head_size)
    place = lax.broadcasted_iota(jnp.int32, (per_group, cache_len), 1)

    att_copies = []
    for step, k in enumerate(heads):
        kv_copies[step][0].wait()
        lanes = pl.ds(pl.multiple_of(k * head_size, head_size), head_size)
        fresh_k = new_key[:, lanes].astype(F32)
        fresh_v = new_value[:, lanes].astype(F32)
        scores, selfs = [], []
        for r in range(rows):
            start = pl.multiple_of(r * kv_count * per_group + k * per_group, per_group)
            q = q_rows[pl.ds(start, per_group), :]
            score = lax.dot_general(
                q.astype(BF16),
                k_buf[step, r],
                (((1,), (1,)), ((), ())),
                preferred_element_type=F32,
            )
            score = jnp.where(place < lengths[r], score * scaling, -jnp.inf)
            scores.append(score)
            selfs.append(jnp.sum(q * fresh_k[r : r + 1], axis=-1, keepdims=True) * scaling)
        score = jnp.concatenate(scores, axis=0)
        self_score = jnp.concatenate(selfs, axis=0)
        highest = jnp.maximum(jnp.max(score, axis=-1, keepdims=True), self_score)
        exponent = jnp.exp(score - highest)
        self_exp = jnp.exp(self_score - highest)
        denominator = jnp.sum(exponent, axis=-1, keepdims=True) + self_exp
        weights = (exponent / denominator).astype(BF16)
        self_weight = (self_exp / denominator).astype(BF16).astype(F32)
        kv_copies[step][1].wait()
        for r in range(rows):
            band = slice(r * per_group, (r + 1) * per_group)
            o_rows[band, :] = (
                jnp.dot(weights[band], v_buf[step, r], preferred_element_type=F32)
                + self_weight[band] * fresh_v[r : r + 1]
            )
        if step == 0:
            pl.semaphore_wait(barrier, n_expert + n_dp - 2)
        last = step == n_expert - 1
        target = att_recv.at[e] if last else att_send.at[step]
        for h in range(per_group):
            target[:, h * head_size : (h + 1) * head_size] = o_rows[
                pl.ds(h, rows, stride=per_group), :
            ].astype(BF16)
        if not last:
            copy = pltpu.make_async_remote_copy(
                src_ref=att_send.at[step],
                dst_ref=att_recv.at[e],
                send_sem=att_ssem.at[step],
                recv_sem=att_rsem.at[e],
                device_id={"expert": k},
                device_id_type=MESH,
            )
            copy.start()
            att_copies.append(copy)

    probs = gate_probs[...]
    probs = probs / jnp.sum(probs, axis=-1, keepdims=True)
    ids = expert_ids[...]
    side_place = lax.broadcasted_iota(jnp.int32, (rows, SIDE), 1)
    weighting = jnp.zeros((rows, SIDE), F32)
    for t in range(ids.shape[1]):
        weighting = weighting + jnp.where(side_place == ids[:, t : t + 1], probs[:, t : t + 1], 0.0)
    mine = e * n_dp + z
    gathered[mine, :, width:] = weighting.astype(BF16)

    for step in range(n_expert - 1):
        src = lax.rem(e + 1 + step, n_expert)
        pltpu.make_async_remote_copy(
            src_ref=att_send.at[step],
            dst_ref=att_recv.at[src],
            send_sem=att_ssem.at[step],
            recv_sem=att_rsem.at[src],
            device_id={"expert": src},
            device_id_type=MESH,
        ).wait_recv()
    left = jnp.concatenate([att_recv[i].astype(F32) for i in range(n_expert)], axis=0).astype(BF16)
    proj_copies = []
    tile = 512
    for n in range(CHUNKS):
        wo_copies[n].wait()

        @pl.loop(0, chunk // tile)
        def _(t):
            cols = pl.ds(pl.multiple_of(n * chunk + t * tile, tile), tile)
            product = jnp.dot(left, wo_buf[:, cols], preferred_element_type=F32)
            for i in range(n_expert):
                proj_own[i, :, cols] = product[i * rows : (i + 1) * rows]

        cols = pl.ds(n * chunk, chunk)
        for step in range(n_expert - 1):
            dst = lax.rem(e + 1 + step, n_expert)
            proj_send[n, step] = proj_own[dst, :, cols].astype(BF16)
            copy = pltpu.make_async_remote_copy(
                src_ref=proj_send.at[n, step],
                dst_ref=proj_recv.at[n, step],
                send_sem=proj_ssem.at[n, step],
                recv_sem=proj_rsem.at[n, step],
                device_id={"expert": dst},
                device_id_type=MESH,
            )
            copy.start()
            proj_copies.append(copy)
    wd_copies = []
    for j in range(local_experts):
        wc = pltpu.make_async_copy(w_down.at[j], wo_buf.at[pl.ds(j * ff, ff), :], wd_sem.at[j])
        wc.start()
        wd_copies.append(wc)

    squares = jnp.zeros((rows, 1), F32)
    for n in range(CHUNKS):
        cols = slice(n * chunk, (n + 1) * chunk)
        total = residual[:, cols].astype(F32) + proj_own[e, :, cols]
        for step in range(n_expert - 1):
            proj_copies[n * (n_expert - 1) + step].wait_recv()
            total = total + proj_recv[n, step].astype(F32)
        total = total.astype(BF16).astype(F32)
        hidden_buf[:, cols] = total
        squares = squares + jnp.sum(total * total, axis=-1, keepdims=True)
    inverse = lax.rsqrt(squares * (1.0 / width) + EPS)
    for n in range(CHUNKS):
        cols = slice(n * chunk, (n + 1) * chunk)
        gathered[mine, :, cols] = (hidden_buf[:, cols] * inverse * norm_gain[:, cols]).astype(BF16)

    def carry(block, kind, slot, device):
        return pltpu.make_async_remote_copy(
            src_ref=gathered.at[block],
            dst_ref=gathered.at[block],
            send_sem=gat_ssem.at[kind, slot],
            recv_sem=gat_rsem.at[block],
            device_id=device,
            device_id_type=MESH,
        )

    def arrive(block):
        carry(block, 0, 0, {"expert": mate}).wait_recv()

    right, left_dp = {"dp": z + 1}, {"dp": z - 1}
    has_right, has_left = z + 1 < n_dp, z > 0
    other, partner = {"expert": across}, {"expert": mate}

    @pl.when(has_right)
    def _():
        carry(mine, 0, 0, right).start()

    @pl.when(has_left)
    def _():
        carry(mine, 1, 0, left_dp).start()

    carry(mine, 2, 0, other).start()
    carry(mine, 4, 0, partner).start()

    def from_side(step, sign):
        kind = 0 if sign < 0 else 1
        there = z + sign * step
        inside = there >= 0 if sign < 0 else there < n_dp
        onward = has_right if sign < 0 else has_left
        target = right if sign < 0 else left_dp

        @pl.when(inside)
        def _():
            block = e * n_dp + there
            arrive(block)

            @pl.when(onward)
            def _():
                carry(block, kind, step, target).start()

            carry(block, 2 + kind, step, other).start()
            carry(block, 4 + kind, step, partner).start()

    def from_across(step, sign):
        kind = 0 if sign < 0 else 1
        there = z + sign * step
        inside = there >= 0 if sign < 0 else there < n_dp

        @pl.when(inside)
        def _():
            block = across * n_dp + there
            arrive(block)
            carry(block, 6 + kind, step, partner).start()

    for step in range(1, n_dp):
        from_side(step, -1)
        from_side(step, 1)
        from_across(step - 1, -1)
        if step > 1:
            from_across(step - 1, 1)
    from_across(n_dp - 1, -1)
    from_across(n_dp - 1, 1)
    mate_across = lax.rem(mate + 2, 4)
    for there in range(n_dp):
        arrive(mate * n_dp + there)
        arrive(mate_across * n_dp + there)

    blocks = n_expert * n_dp
    all_rows = blocks * rows
    for copy in gu_copies:
        copy.wait()
    all_weights = gathered[:, :, width:].astype(F32).reshape(all_rows, SIDE)
    all_place = lax.broadcasted_iota(jnp.int32, (all_rows, SIDE), 1)

    @pl.loop(0, local_experts)
    def _(j):
        cols = pl.ds(pl.multiple_of(j * (2 * ff), 2 * ff), 2 * ff)
        total = jnp.zeros((all_rows, 2 * ff), F32)
        for n in range(CHUNKS):
            ks = slice(n * chunk, (n + 1) * chunk)
            x = gathered[:, :, ks].reshape(all_rows, chunk)
            total = total + jnp.dot(x, gu_buf[ks, cols], preferred_element_type=F32)
        gate_out = total[:, :ff]
        up_out = total[:, ff:]
        column = jnp.sum(
            jnp.where(all_place == e * local_experts + j, all_weights, 0.0), axis=-1, keepdims=True
        )
        activated = gate_out / (1.0 + jnp.exp(-gate_out)) * up_out * column
        acts[:, pl.ds(pl.multiple_of(j * ff, ff), ff)] = activated.astype(BF16)

    for copy in wd_copies:
        copy.wait()

    def stage(send, recv, ssem, rsem, device):
        copy = pltpu.make_async_remote_copy(
            src_ref=send, dst_ref=recv, send_sem=ssem, recv_sem=rsem, device_id=device, device_id_type=MESH
        )
        copy.start()
        return copy

    c1, c2, c3 = [], [], []

    def down(n):
        @pl.loop(0, chunk // tile)
        def _(t):
            cols = pl.ds(pl.multiple_of(n * chunk + t * tile, tile), tile)
            here = pl.ds(pl.multiple_of(t * tile, tile), tile)
            product = jnp.dot(
                acts[...], wo_buf[: local_experts * ff, cols], preferred_element_type=F32
            )
            part[n, :, :, :, :, here] = product.reshape(2, 2, n_dp, rows, tile)

        s1[n] = part[n, :, 1 - core].astype(BF16)
        c1.append(stage(s1.at[n], r1.at[n], s1_sem.at[n], r1_sem.at[n], {"expert": mate}))

    def second(n):
        c1[n].wait_recv()
        s2[n] = (part[n, 1 - y, core] + r1[n, 1 - y].astype(F32)).astype(BF16)
        c2.append(stage(s2.at[n], r2.at[n], s2_sem.at[n], r2_sem.at[n], {"expert": across}))
        part[n, y, core] = part[n, y, core] + r1[n, y].astype(F32)

    def third(n):
        c2[n].wait_recv()
        for step in range(1, n_dp):
            there = lax.rem(z + step, n_dp)
            s3[n, step - 1] = (part[n, y, core, there] + r2[n, there].astype(F32)).astype(BF16)
            c3.append(
                stage(
                    s3.at[n, step - 1],
                    r3.at[n, step - 1],
                    s3_sem.at[n, step - 1],
                    r3_sem.at[n, step - 1],
                    {"dp": there},
                )
            )

    def finish(n):
        cols = slice(n * chunk, (n + 1) * chunk)
        total = part[n, y, core, z] + r2[n, z].astype(F32)
        for step in range(n_dp - 1):
            c3[n * (n_dp - 1) + step].wait_recv()
            total = total + r3[n, step].astype(F32)
        out[:, cols] = (hidden_buf[:, cols] + total).astype(BF16)

    for n in range(CHUNKS + 2):
        if n < CHUNKS:
            down(n)
        if 0 <= n - 1 < CHUNKS:
            second(n - 1)
        if 0 <= n - 2 < CHUNKS:
            third(n - 2)
    for n in range(CHUNKS):
        finish(n)
    for copy in att_copies + proj_copies + c1 + c2 + c3:
        copy.wait_send()

    def drain(step, sign):
        kind = 0 if sign < 0 else 1
        there = z + sign * step
        inside = there >= 0 if sign < 0 else there < n_dp
        onward = has_right if sign < 0 else has_left

        @pl.when(inside)
        def _():
            @pl.when(onward)
            def _():
                carry(e * n_dp + there, kind, step, partner).wait_send()

            if step or sign < 0:
                carry(e * n_dp + there, 2 + kind, step, partner).wait_send()
                carry(e * n_dp + there, 4 + kind, step, partner).wait_send()
                carry(across * n_dp + there, 6 + kind, step, partner).wait_send()

    for step in range(n_dp):
        drain(step, -1)
        drain(step, 1)


def per_device_fused(sizes, *args):
    n_expert, n_dp = sizes["expert"], sizes["dp"]
    query, key_cache, w_gate = args[0], args[1], args[11]
    residual, out_proj = args[6], args[7]
    rows, kv_count, cache_len, head_size = key_cache.shape
    width = residual.shape[1]
    local_experts, _, ff = w_gate.shape
    feat = out_proj.shape[0]
    weight_bytes = 2 * (out_proj.size + 2 * w_gate.size + 2 * key_cache.size)
    fits = (
        n_expert == 4
        and kv_count == n_expert
        and ff % 128 == 0
        and local_experts * ff <= feat
        and rows == 8
        and weight_bytes <= 48 * MIB
    )
    if not fits:
        return per_device(*args)
    per_group = query.shape[1] // (kv_count * head_size)
    blocks = n_expert * n_dp
    chunk = width // CHUNKS
    dma = pltpu.SemaphoreType.DMA
    vmem, anyspace = pl.BlockSpec(memory_space=pltpu.VMEM), pl.BlockSpec(memory_space=pl.ANY)
    smem = pl.BlockSpec(memory_space=pltpu.SMEM)
    specs = [vmem, anyspace, anyspace, vmem, vmem, smem, vmem, anyspace, vmem, vmem, vmem]
    specs += [anyspace] * 3
    operands = list(args)
    operands[8] = args[8].reshape(1, width)
    flops = 2 * blocks * rows * 3 * w_gate.size + 2 * n_expert * rows * out_proj.size
    return pl.pallas_call(
        functools.partial(fused_kernel, n_expert, n_dp),
        out_shape=jax.ShapeDtypeStruct((rows, width), BF16),
        in_specs=specs,
        out_specs=vmem,
        scratch_shapes=[
            pltpu.VMEM((kv_count, rows, cache_len, head_size), BF16),
            pltpu.VMEM((kv_count, rows, cache_len, head_size), BF16),
            pltpu.VMEM((feat, width), BF16),
            pltpu.VMEM((width, 2 * local_experts * ff), BF16),
            pltpu.VMEM((rows * kv_count * per_group, head_size), F32),
            pltpu.VMEM((rows * per_group, head_size), F32),
            pltpu.VMEM((n_expert - 1, rows, feat), BF16),
            pltpu.VMEM((n_expert, rows, feat), BF16),
            pltpu.VMEM((CHUNKS, n_expert - 1, rows, chunk), BF16),
            pltpu.VMEM((CHUNKS, n_expert - 1, rows, chunk), BF16),
            pltpu.VMEM((n_expert, rows, width), F32),
            pltpu.VMEM((rows, width), F32),
            pltpu.VMEM((blocks, rows, width + SIDE), BF16),
            pltpu.VMEM((blocks * rows, local_experts * ff), BF16),
            pltpu.VMEM((CHUNKS, 2, 2, n_dp, rows, chunk), F32),
            pltpu.VMEM((CHUNKS, 2, n_dp, rows, chunk), BF16),
            pltpu.VMEM((CHUNKS, 2, n_dp, rows, chunk), BF16),
            pltpu.VMEM((CHUNKS, n_dp, rows, chunk), BF16),
            pltpu.VMEM((CHUNKS, n_dp, rows, chunk), BF16),
            pltpu.VMEM((CHUNKS, n_dp - 1, rows, chunk), BF16),
            pltpu.VMEM((CHUNKS, n_dp - 1, rows, chunk), BF16),
            dma((2, n_expert)),
            dma((CHUNKS,)),
            dma((local_experts, 2)),
            dma((local_experts,)),
            dma((n_expert - 1,)),
            dma((n_expert,)),
            dma((CHUNKS, n_expert - 1)),
            dma((CHUNKS, n_expert - 1)),
            dma((8, n_dp)),
            dma((blocks,)),
            dma((CHUNKS,)),
            dma((CHUNKS,)),
            dma((CHUNKS,)),
            dma((CHUNKS,)),
            dma((CHUNKS, n_dp - 1)),
            dma((CHUNKS, n_dp - 1)),
        ],
        compiler_params=pltpu.CompilerParams(
            collective_id=0, has_side_effects=True, vmem_limit_bytes=60 * MIB
        ),
        cost_estimate=pl.CostEstimate(
            flops=flops,
            bytes_accessed=2 * (out_proj.size + 3 * w_gate.size + 2 * key_cache.size),
            transcendentals=0,
        ),
    )(*operands)


def solution(mesh):
    return jax.shard_map(
        functools.partial(per_device_fused, dict(mesh.shape)),
        mesh=mesh,
        in_specs=(
            P(("group", "expert", "dp"), None),
            P(("group", "expert", "dp"), None, None, None),
            P(("group", "expert", "dp"), None, None, None),
            P(("group", "expert", "dp"), None),
            P(("group", "expert", "dp"), None),
            P(("group", "expert", "dp")),
            P(("group", "expert", "dp"), None),
            P("expert", None),
            P(),
            P(("group", "expert", "dp"), None),
            P(("group", "expert", "dp"), None),
            P("expert", None, "dp"),
            P("expert", None, "dp"),
            P("expert", "dp", None),
        ),
        out_specs=P(("group", "expert", "dp"), None),
        check_vma=False,
    )
```

```python
import functools
import math

import jax
import jax.numpy as jnp
from jax import lax
from jax.experimental import pallas as pl
from jax.experimental.pallas import tpu as pltpu
from jax.sharding import PartitionSpec as P

EPS = 1e-06


def attend(query, key_cache, value_cache, new_key, new_value, lengths):
    row_count = query.shape[0]
    kv_count = key_cache.shape[1]
    cache_len = key_cache.shape[2]
    head_size = key_cache.shape[3]
    per_group = query.shape[1] // (kv_count * head_size)
    queries = query.reshape(row_count, kv_count, per_group, head_size)
    scaling = 1.0 / math.sqrt(head_size)
    scores = (
        jnp.einsum("rkgd,rkcd->rkgc", queries, key_cache, preferred_element_type=jnp.float32)
        * scaling
    )
    fresh_keys = new_key.reshape(row_count, kv_count, head_size)
    self_score = (
        jnp.einsum("rkgd,rkd->rkg", queries, fresh_keys, preferred_element_type=jnp.float32)
        * scaling
    )
    usable = jnp.arange(cache_len, dtype=jnp.int32)[None, :] < lengths[:, None]
    scores = jnp.where(usable[:, None, None, :], scores, -jnp.inf)
    highest = jnp.maximum(jnp.max(scores, axis=-1), self_score)
    exponent = jnp.exp(scores - highest[..., None])
    self_exp = jnp.exp(self_score - highest)
    denominator = jnp.sum(exponent, axis=-1) + self_exp
    weights = (exponent / denominator[..., None]).astype(jnp.bfloat16)
    self_weight = lax.optimization_barrier((self_exp / denominator).astype(jnp.bfloat16)).astype(
        jnp.float32
    )
    fresh_values = new_value.astype(jnp.float32).reshape(row_count, kv_count, head_size)
    attended = jnp.einsum(
        "rkgc,rkcd->rkgd", weights, value_cache, preferred_element_type=jnp.float32
    )
    attended = attended + self_weight[..., None] * fresh_values[:, :, None, :]
    return attended.astype(jnp.bfloat16).reshape(row_count, per_group * kv_count * head_size)


def routing(expert_ids, gate_probs, expert_total):
    normalized = gate_probs / jnp.sum(gate_probs, axis=-1, keepdims=True)
    matches = expert_ids[:, :, None] == jnp.arange(expert_total, dtype=jnp.int32)[None, None, :]
    return jnp.sum(jnp.where(matches, normalized[:, :, None], 0.0), axis=1).astype(jnp.bfloat16)


def expert_apply(row_block, weight_block, w_gate, w_up):
    gate_out = jnp.einsum("md,kdf->mkf", row_block, w_gate, preferred_element_type=jnp.float32)
    up_out = jnp.einsum("md,kdf->mkf", row_block, w_up, preferred_element_type=jnp.float32)
    activated = (
        jax.nn.silu(gate_out) * up_out * weight_block.astype(jnp.float32)[:, :, None]
    ).astype(jnp.bfloat16)
    return activated.reshape(row_block.shape[0], -1)


def per_device(
    query,
    key_cache,
    value_cache,
    new_key,
    new_value,
    lengths,
    residual,
    out_proj,
    norm_gain,
    expert_ids,
    gate_probs,
    w_gate,
    w_up,
    w_down,
):
    width = residual.shape[1]
    local_experts = w_gate.shape[0]
    n_expert = lax.axis_size("expert")
    down_flat = w_down.reshape(-1, width)
    attended = attend(query, key_cache, value_cache, new_key, new_value, lengths)
    received = lax.all_to_all(attended, "expert", split_axis=1, concat_axis=0, tiled=True)
    projected = lax.psum_scatter(
        jnp.dot(received, out_proj, preferred_element_type=jnp.float32),
        "expert",
        scatter_dimension=0,
        tiled=True,
    )
    hidden = (residual.astype(jnp.float32) + projected).astype(jnp.bfloat16)
    hidden_wide = hidden.astype(jnp.float32)
    mean_square = jnp.mean(hidden_wide * hidden_wide, axis=-1, keepdims=True)
    normed = (hidden_wide * lax.rsqrt(mean_square + EPS) * norm_gain).astype(jnp.bfloat16)
    expert_total = local_experts * n_expert
    weighting = routing(expert_ids, gate_probs, expert_total)
    all_rows, all_weighting = (
        lax.all_gather(normed, ("expert", "dp"), axis=0, tiled=True),
        lax.all_gather(weighting, ("expert", "dp"), axis=0, tiled=True),
    )
    first_expert = lax.axis_index("expert") * local_experts
    local_weighting = lax.dynamic_slice_in_dim(all_weighting, first_expert, local_experts, 1)
    activated = expert_apply(all_rows, local_weighting, w_gate, w_up)
    expert_sum = lax.psum_scatter(
        jnp.dot(activated, down_flat, preferred_element_type=jnp.float32),
        ("expert", "dp"),
        scatter_dimension=0,
        tiled=True,
    )
    return (hidden_wide + expert_sum).astype(jnp.bfloat16)


MESH = pl.DeviceIdType.MESH
F32 = jnp.float32
BF16 = jnp.bfloat16
CHUNKS = 4
SIDE = 128
MIB = 1 << 20


def fused_kernel(
    n_expert,
    n_dp,
    query,
    key_cache,
    value_cache,
    new_key,
    new_value,
    lengths,
    residual,
    out_proj,
    norm_gain,
    expert_ids,
    gate_probs,
    w_gate,
    w_up,
    w_down,
    out,
    k_buf,
    v_buf,
    wo_buf,
    gu_buf,
    q_rows,
    o_rows,
    att_send,
    att_recv,
    proj_send,
    proj_recv,
    proj_own,
    hidden_buf,
    gathered,
    acts,
    part,
    s1,
    r1,
    s2,
    r2,
    s3,
    r3,
    kv_sem,
    wo_sem,
    gu_sem,
    wd_sem,
    att_ssem,
    att_rsem,
    proj_ssem,
    proj_rsem,
    gat_ssem,
    gat_rsem,
    s1_sem,
    r1_sem,
    s2_sem,
    r2_sem,
    s3_sem,
    r3_sem,
):
    rows, kv_count, cache_len, head_size = key_cache.shape
    per_group = query.shape[1] // (kv_count * head_size)
    width = residual.shape[1]
    feat = att_send.shape[2]
    local_experts, _, ff = w_gate.shape
    chunk = width // CHUNKS
    e = lax.axis_index("expert")
    z = lax.axis_index("dp")
    core = lax.rem(e, 2)
    y = lax.div(e, 2)
    mate = e + 1 - 2 * core
    across = lax.rem(e + 2, 4)

    barrier = pltpu.get_barrier_semaphore()
    for step in range(1, n_expert):
        pl.semaphore_signal(
            barrier, inc=1, device_id={"expert": lax.rem(e + step, n_expert)}, device_id_type=MESH
        )
    for step in range(1, n_dp):
        pl.semaphore_signal(
            barrier, inc=1, device_id={"dp": lax.rem(z + step, n_dp)}, device_id_type=MESH
        )

    heads = [lax.rem(e + 1 + step, n_expert) for step in range(n_expert)]
    kv_copies = []
    for step, k in enumerate(heads):
        kc = pltpu.make_async_copy(key_cache.at[:, k], k_buf.at[step], kv_sem.at[0, step])
        vc = pltpu.make_async_copy(value_cache.at[:, k], v_buf.at[step], kv_sem.at[1, step])
        kc.start()
        vc.start()
        kv_copies.append((kc, vc))
    wo_copies = []
    for n in range(CHUNKS):
        cols = pl.ds(n * chunk, chunk)
        wc = pltpu.make_async_copy(out_proj.at[:, cols], wo_buf.at[:, cols], wo_sem.at[n])
        wc.start()
        wo_copies.append(wc)
    gu_copies = []
    for j in range(local_experts):
        for t, w in enumerate((w_gate, w_up)):
            gc = pltpu.make_async_copy(
                w.at[j], gu_buf.at[:, pl.ds((2 * j + t) * ff, ff)], gu_sem.at[j, t]
            )
            gu_copies.append(gc)

    for h in range(kv_count * per_group):
        q_rows[pl.ds(h, rows, stride=kv_count * per_group), :] = query[
            :, h * head_size : (h + 1) * head_size
        ].astype(F32)
    scaling = 1.0 / math.sqrt(head_size)
    place = lax.broadcasted_iota(jnp.int32, (per_group, cache_len), 1)

    att_copies = []
    for step, k in enumerate(heads):
        kv_copies[step][0].wait()
        lanes = pl.ds(pl.multiple_of(k * head_size, head_size), head_size)
        fresh_k = new_key[:, lanes].astype(F32)
        fresh_v = new_value[:, lanes].astype(F32)
        scores, selfs = [], []
        for r in range(rows):
            start = pl.multiple_of(r * kv_count * per_group + k * per_group, per_group)
            q = q_rows[pl.ds(start, per_group), :]
            score = lax.dot_general(
                q.astype(BF16),
                k_buf[step, r],
                (((1,), (1,)), ((), ())),
                preferred_element_type=F32,
            )
            score = jnp.where(place < lengths[r], score * scaling, -jnp.inf)
            scores.append(score)
            selfs.append(jnp.sum(q * fresh_k[r : r + 1], axis=-1, keepdims=True) * scaling)
        score = jnp.concatenate(scores, axis=0)
        self_score = jnp.concatenate(selfs, axis=0)
        highest = jnp.maximum(jnp.max(score, axis=-1, keepdims=True), self_score)
        exponent = jnp.exp(score - highest)
        self_exp = jnp.exp(self_score - highest)
        denominator = jnp.sum(exponent, axis=-1, keepdims=True) + self_exp
        weights = (exponent / denominator).astype(BF16)
        self_weight = (self_exp / denominator).astype(BF16).astype(F32)
        kv_copies[step][1].wait()
        for r in range(rows):
            band = slice(r * per_group, (r + 1) * per_group)
            o_rows[band, :] = (
                jnp.dot(weights[band], v_buf[step, r], preferred_element_type=F32)
                + self_weight[band] * fresh_v[r : r + 1]
            )
        if step == 0:
            pl.semaphore_wait(barrier, n_expert + n_dp - 2)
        last = step == n_expert - 1
        target = att_recv.at[e] if last else att_send.at[step]
        for h in range(per_group):
            target[:, h * head_size : (h + 1) * head_size] = o_rows[
                pl.ds(h, rows, stride=per_group), :
            ].astype(BF16)
        if not last:
            copy = pltpu.make_async_remote_copy(
                src_ref=att_send.at[step],
                dst_ref=att_recv.at[e],
                send_sem=att_ssem.at[step],
                recv_sem=att_rsem.at[e],
                device_id={"expert": k},
                device_id_type=MESH,
            )
            copy.start()
            att_copies.append(copy)

    for copy in gu_copies:
        copy.start()

    probs = gate_probs[...]
    probs = probs / jnp.sum(probs, axis=-1, keepdims=True)
    ids = expert_ids[...]
    side_place = lax.broadcasted_iota(jnp.int32, (rows, SIDE), 1)
    weighting = jnp.zeros((rows, SIDE), F32)
    for t in range(ids.shape[1]):
        weighting = weighting + jnp.where(side_place == ids[:, t : t + 1], probs[:, t : t + 1], 0.0)
    mine = e * n_dp + z
    gathered[mine, :, width:] = weighting.astype(BF16)

    for step in range(n_expert - 1):
        src = lax.rem(e + 1 + step, n_expert)
        pltpu.make_async_remote_copy(
            src_ref=att_send.at[step],
            dst_ref=att_recv.at[src],
            send_sem=att_ssem.at[step],
            recv_sem=att_rsem.at[src],
            device_id={"expert": src},
            device_id_type=MESH,
        ).wait_recv()
    left = jnp.concatenate([att_recv[i].astype(F32) for i in range(n_expert)], axis=0).astype(BF16)
    proj_copies = []
    tile = 512
    for n in range(CHUNKS):
        wo_copies[n].wait()

        @pl.loop(0, chunk // tile)
        def _(t):
            cols = pl.ds(pl.multiple_of(n * chunk + t * tile, tile), tile)
            product = jnp.dot(left, wo_buf[:, cols], preferred_element_type=F32)
            for i in range(n_expert):
                proj_own[i, :, cols] = product[i * rows : (i + 1) * rows]

        cols = pl.ds(n * chunk, chunk)
        for step in range(n_expert - 1):
            dst = lax.rem(e + 1 + step, n_expert)
            proj_send[n, step] = proj_own[dst, :, cols].astype(BF16)
            copy = pltpu.make_async_remote_copy(
                src_ref=proj_send.at[n, step],
                dst_ref=proj_recv.at[n, step],
                send_sem=proj_ssem.at[n, step],
                recv_sem=proj_rsem.at[n, step],
                device_id={"expert": dst},
                device_id_type=MESH,
            )
            copy.start()
            proj_copies.append(copy)
    wd_copies = []
    for j in range(local_experts):
        wc = pltpu.make_async_copy(w_down.at[j], wo_buf.at[pl.ds(j * ff, ff), :], wd_sem.at[j])
        wc.start()
        wd_copies.append(wc)

    squares = jnp.zeros((rows, 1), F32)
    for n in range(CHUNKS):
        cols = slice(n * chunk, (n + 1) * chunk)
        total = residual[:, cols].astype(F32) + proj_own[e, :, cols]
        for step in range(n_expert - 1):
            proj_copies[n * (n_expert - 1) + step].wait_recv()
            total = total + proj_recv[n, step].astype(F32)
        total = total.astype(BF16).astype(F32)
        hidden_buf[:, cols] = total
        squares = squares + jnp.sum(total * total, axis=-1, keepdims=True)
    inverse = lax.rsqrt(squares * (1.0 / width) + EPS)
    for n in range(CHUNKS):
        cols = slice(n * chunk, (n + 1) * chunk)
        gathered[mine, :, cols] = (hidden_buf[:, cols] * inverse * norm_gain[:, cols]).astype(BF16)

    def carry(block, kind, slot, device):
        return pltpu.make_async_remote_copy(
            src_ref=gathered.at[block],
            dst_ref=gathered.at[block],
            send_sem=gat_ssem.at[kind, slot],
            recv_sem=gat_rsem.at[block],
            device_id=device,
            device_id_type=MESH,
        )

    def arrive(block):
        carry(block, 0, 0, {"expert": mate}).wait_recv()

    right, left_dp = {"dp": z + 1}, {"dp": z - 1}
    has_right, has_left = z + 1 < n_dp, z > 0
    other, partner = {"expert": across}, {"expert": mate}

    @pl.when(has_right)
    def _():
        carry(mine, 0, 0, right).start()

    @pl.when(has_left)
    def _():
        carry(mine, 1, 0, left_dp).start()

    carry(mine, 2, 0, other).start()
    carry(mine, 4, 0, partner).start()

    def from_side(step, sign):
        kind = 0 if sign < 0 else 1
        there = z + sign * step
        inside = there >= 0 if sign < 0 else there < n_dp
        onward = has_right if sign < 0 else has_left
        target = right if sign < 0 else left_dp

        @pl.when(inside)
        def _():
            block = e * n_dp + there
            arrive(block)

            @pl.when(onward)
            def _():
                carry(block, kind, step, target).start()

            carry(block, 2 + kind, step, other).start()
            carry(block, 4 + kind, step, partner).start()

    def from_across(step, sign):
        kind = 0 if sign < 0 else 1
        there = z + sign * step
        inside = there >= 0 if sign < 0 else there < n_dp

        @pl.when(inside)
        def _():
            block = across * n_dp + there
            arrive(block)
            carry(block, 6 + kind, step, partner).start()

    for step in range(1, n_dp):
        from_side(step, -1)
        from_side(step, 1)
        from_across(step - 1, -1)
        if step > 1:
            from_across(step - 1, 1)
    from_across(n_dp - 1, -1)
    from_across(n_dp - 1, 1)
    mate_across = lax.rem(mate + 2, 4)
    for there in range(n_dp):
        arrive(mate * n_dp + there)
        arrive(mate_across * n_dp + there)

    blocks = n_expert * n_dp
    all_rows = blocks * rows
    for copy in gu_copies:
        copy.wait()
    all_weights = gathered[:, :, width:].astype(F32).reshape(all_rows, SIDE)
    all_place = lax.broadcasted_iota(jnp.int32, (all_rows, SIDE), 1)

    @pl.loop(0, local_experts)
    def _(j):
        cols = pl.ds(pl.multiple_of(j * (2 * ff), 2 * ff), 2 * ff)
        total = jnp.zeros((all_rows, 2 * ff), F32)
        for n in range(CHUNKS):
            ks = slice(n * chunk, (n + 1) * chunk)
            x = gathered[:, :, ks].reshape(all_rows, chunk)
            total = total + jnp.dot(x, gu_buf[ks, cols], preferred_element_type=F32)
        gate_out = total[:, :ff]
        up_out = total[:, ff:]
        column = jnp.sum(
            jnp.where(all_place == e * local_experts + j, all_weights, 0.0), axis=-1, keepdims=True
        )
        activated = gate_out / (1.0 + jnp.exp(-gate_out)) * up_out * column
        acts[:, pl.ds(pl.multiple_of(j * ff, ff), ff)] = activated.astype(BF16)

    for copy in wd_copies:
        copy.wait()

    def stage(send, recv, ssem, rsem, device):
        copy = pltpu.make_async_remote_copy(
            src_ref=send, dst_ref=recv, send_sem=ssem, recv_sem=rsem, device_id=device, device_id_type=MESH
        )
        copy.start()
        return copy

    c1, c2, c3 = [], [], []

    def down(n):
        @pl.loop(0, chunk // tile)
        def _(t):
            cols = pl.ds(pl.multiple_of(n * chunk + t * tile, tile), tile)
            here = pl.ds(pl.multiple_of(t * tile, tile), tile)
            product = jnp.dot(
                acts[...], wo_buf[: local_experts * ff, cols], preferred_element_type=F32
            )
            part[n, :, :, :, :, here] = product.reshape(2, 2, n_dp, rows, tile)

        s1[n] = part[n, :, 1 - core].astype(BF16)
        c1.append(stage(s1.at[n], r1.at[n], s1_sem.at[n], r1_sem.at[n], {"expert": mate}))

    def second(n):
        c1[n].wait_recv()
        s2[n] = (part[n, 1 - y, core] + r1[n, 1 - y].astype(F32)).astype(BF16)
        c2.append(stage(s2.at[n], r2.at[n], s2_sem.at[n], r2_sem.at[n], {"expert": across}))
        part[n, y, core] = part[n, y, core] + r1[n, y].astype(F32)

    def third(n):
        c2[n].wait_recv()
        for step in range(1, n_dp):
            there = lax.rem(z + step, n_dp)
            s3[n, step - 1] = (part[n, y, core, there] + r2[n, there].astype(F32)).astype(BF16)
            c3.append(
                stage(
                    s3.at[n, step - 1],
                    r3.at[n, step - 1],
                    s3_sem.at[n, step - 1],
                    r3_sem.at[n, step - 1],
                    {"dp": there},
                )
            )

    def finish(n):
        cols = slice(n * chunk, (n + 1) * chunk)
        total = part[n, y, core, z] + r2[n, z].astype(F32)
        for step in range(n_dp - 1):
            c3[n * (n_dp - 1) + step].wait_recv()
            total = total + r3[n, step].astype(F32)
        out[:, cols] = (hidden_buf[:, cols] + total).astype(BF16)

    for n in range(CHUNKS + 2):
        if n < CHUNKS:
            down(n)
        if 0 <= n - 1 < CHUNKS:
            second(n - 1)
        if 0 <= n - 2 < CHUNKS:
            third(n - 2)
    for n in range(CHUNKS):
        finish(n)
    for copy in att_copies + proj_copies + c1 + c2 + c3:
        copy.wait_send()

    def drain(step, sign):
        kind = 0 if sign < 0 else 1
        there = z + sign * step
        inside = there >= 0 if sign < 0 else there < n_dp
        onward = has_right if sign < 0 else has_left

        @pl.when(inside)
        def _():
            @pl.when(onward)
            def _():
                carry(e * n_dp + there, kind, step, partner).wait_send()

            if step or sign < 0:
                carry(e * n_dp + there, 2 + kind, step, partner).wait_send()
                carry(e * n_dp + there, 4 + kind, step, partner).wait_send()
                carry(across * n_dp + there, 6 + kind, step, partner).wait_send()

    for step in range(n_dp):
        drain(step, -1)
        drain(step, 1)


def per_device_fused(sizes, *args):
    n_expert, n_dp = sizes["expert"], sizes["dp"]
    query, key_cache, w_gate = args[0], args[1], args[11]
    residual, out_proj = args[6], args[7]
    rows, kv_count, cache_len, head_size = key_cache.shape
    width = residual.shape[1]
    local_experts, _, ff = w_gate.shape
    feat = out_proj.shape[0]
    weight_bytes = 2 * (out_proj.size + 2 * w_gate.size + 2 * key_cache.size)
    fits = (
        n_expert == 4
        and kv_count == n_expert
        and ff % 128 == 0
        and local_experts * ff <= feat
        and rows == 8
        and weight_bytes <= 48 * MIB
    )
    if not fits:
        return per_device(*args)
    per_group = query.shape[1] // (kv_count * head_size)
    blocks = n_expert * n_dp
    chunk = width // CHUNKS
    dma = pltpu.SemaphoreType.DMA
    vmem, anyspace = pl.BlockSpec(memory_space=pltpu.VMEM), pl.BlockSpec(memory_space=pl.ANY)
    smem = pl.BlockSpec(memory_space=pltpu.SMEM)
    specs = [vmem, anyspace, anyspace, vmem, vmem, smem, vmem, anyspace, vmem, vmem, vmem]
    specs += [anyspace] * 3
    operands = list(args)
    operands[8] = args[8].reshape(1, width)
    flops = 2 * blocks * rows * 3 * w_gate.size + 2 * n_expert * rows * out_proj.size
    return pl.pallas_call(
        functools.partial(fused_kernel, n_expert, n_dp),
        out_shape=jax.ShapeDtypeStruct((rows, width), BF16),
        in_specs=specs,
        out_specs=vmem,
        scratch_shapes=[
            pltpu.VMEM((kv_count, rows, cache_len, head_size), BF16),
            pltpu.VMEM((kv_count, rows, cache_len, head_size), BF16),
            pltpu.VMEM((feat, width), BF16),
            pltpu.VMEM((width, 2 * local_experts * ff), BF16),
            pltpu.VMEM((rows * kv_count * per_group, head_size), F32),
            pltpu.VMEM((rows * per_group, head_size), F32),
            pltpu.VMEM((n_expert - 1, rows, feat), BF16),
            pltpu.VMEM((n_expert, rows, feat), BF16),
            pltpu.VMEM((CHUNKS, n_expert - 1, rows, chunk), BF16),
            pltpu.VMEM((CHUNKS, n_expert - 1, rows, chunk), BF16),
            pltpu.VMEM((n_expert, rows, width), F32),
            pltpu.VMEM((rows, width), F32),
            pltpu.VMEM((blocks, rows, width + SIDE), BF16),
            pltpu.VMEM((blocks * rows, local_experts * ff), BF16),
            pltpu.VMEM((CHUNKS, 2, 2, n_dp, rows, chunk), F32),
            pltpu.VMEM((CHUNKS, 2, n_dp, rows, chunk), BF16),
            pltpu.VMEM((CHUNKS, 2, n_dp, rows, chunk), BF16),
            pltpu.VMEM((CHUNKS, n_dp, rows, chunk), BF16),
            pltpu.VMEM((CHUNKS, n_dp, rows, chunk), BF16),
            pltpu.VMEM((CHUNKS, n_dp - 1, rows, chunk), BF16),
            pltpu.VMEM((CHUNKS, n_dp - 1, rows, chunk), BF16),
            dma((2, n_expert)),
            dma((CHUNKS,)),
            dma((local_experts, 2)),
            dma((local_experts,)),
            dma((n_expert - 1,)),
            dma((n_expert,)),
            dma((CHUNKS, n_expert - 1)),
            dma((CHUNKS, n_expert - 1)),
            dma((8, n_dp)),
            dma((blocks,)),
            dma((CHUNKS,)),
            dma((CHUNKS,)),
            dma((CHUNKS,)),
            dma((CHUNKS,)),
            dma((CHUNKS, n_dp - 1)),
            dma((CHUNKS, n_dp - 1)),
        ],
        compiler_params=pltpu.CompilerParams(
            collective_id=0, has_side_effects=True, vmem_limit_bytes=60 * MIB
        ),
        cost_estimate=pl.CostEstimate(
            flops=flops,
            bytes_accessed=2 * (out_proj.size + 3 * w_gate.size + 2 * key_cache.size),
            transcendentals=0,
        ),
    )(*operands)


def solution(mesh):
    return jax.shard_map(
        functools.partial(per_device_fused, dict(mesh.shape)),
        mesh=mesh,
        in_specs=(
            P(("group", "expert", "dp"), None),
            P(("group", "expert", "dp"), None, None, None),
            P(("group", "expert", "dp"), None, None, None),
            P(("group", "expert", "dp"), None),
            P(("group", "expert", "dp"), None),
            P(("group", "expert", "dp")),
            P(("group", "expert", "dp"), None),
            P("expert", None),
            P(),
            P(("group", "expert", "dp"), None),
            P(("group", "expert", "dp"), None),
            P("expert", None, "dp"),
            P("expert", None, "dp"),
            P("expert", "dp", None),
        ),
        out_specs=P(("group", "expert", "dp"), None),
        check_vma=False,
    )
```
